128 devices in a mesh: node: 8 (over z, core), local: 16 (over x, y).
Axes of the slice: x: 4, y: 4, z: 4, core: 2. Of those that a mesh axis runs over, the one named last changes fastest.
Arguments:
- saved_input: bfloat16 [4096, 3584], P('local'), may hold values from -6 to 6
- out_grad: bfloat16 [4096, 3584], P('local'), may hold values from -6 to 6
- routes: int32 [4096, 2], P('local'), may hold values from 0 to 15, all different within a row; in each aligned block of 256 rows (0 to 255, 256 to 511, ...) at most 64 rows name the same one
- gates: bfloat16 [4096, 2], P('local'), may hold values from 0.049804688 to 1
- gate_weight: bfloat16 [16, 3584, 2048], P('local', None, 'node'), may hold values from -0.09375 to 0.09375
- up_weight: bfloat16 [16, 3584, 2048], P('local', None, 'node'), may hold values from -0.09375 to 0.09375
- down_weight: bfloat16 [16, 2048, 3584], P('local', 'node'), may hold values from -0.125 to 0.125
Outputs:
- grad_input: bfloat16 [4096, 3584], P('local', 'node')
- grad_gates: float32 [4096, 2], P('local')
- grad_gate_weight: float32 [16, 3584, 2048], P('local', None, 'node')
- grad_up_weight: float32 [16, 3584, 2048], P('local', None, 'node')
- grad_down_weight: float32 [16, 2048, 3584], P('local', 'node')
The draws below stay inside these ranges and needn't reach their ends.
Inputs may be any that keep to these rules, and one draw needn't show every extreme that they name: `routes`: the 2 experts of a token differ. In each aligned block of 256 tokens (the tokens on one device along local) no expert is chosen by more than 64 tokens, and some expert is chosen by exactly 64.
All inputs are finite; a program needn't handle non-finite values.
Results may differ from the reference program's by a relative error of at most 0.0049.
Values may be sent and summed in bfloat16 or wider, within the bound.
A program may use at most 192 MiB of HBM per device.

```python
import math
import jax
import jax.numpy as jnp
import numpy as np
from jax import lax

D = 3584
H = 2048
TOPK = 2
TOK_DEV = 256
EXPERTS = 16
TOKENS = 4096
CAP = 64
N_LOCAL = 16


def level_of(key, shape, pieces, low, largest):
    level = 1.0
    for position, shards_of in pieces:
        heights = jax.random.uniform(jax.random.fold_in(jax.random.fold_in(key, 6), position), (shards_of,), jnp.float32, low / len(pieces), largest / len(pieces))
        level = level * jnp.repeat(jnp.exp(heights), shape[position] // shards_of).reshape((-1,) + (1,) * (len(shape) - 1 - position))
    return level


def shared_out(own_key, own, number, rows, count, top, reach, lean):
    sequence = jax.random.permutation(own_key, count)
    heavy_load, usual = portions_of(count, rows * top, reach, lean, True), portions_of(count, rows * top, reach, lean, False)
    places = jnp.arange(count)

    def named(sizes, rotation):
        used = int((sizes > 0).sum())
        fixed = max(1, used // 4)
        shifted = fixed + (places - fixed + rotation * (used - fixed)) % max(1, count - fixed)
        return jnp.zeros((count,), jnp.int32).at[sequence[jnp.where(places < fixed, places, shifted)]].set(jnp.asarray(sizes, jnp.int32))

    sizes = jnp.where(number % 4 == 0, named(heavy_load, number // 4), named(usual, number - number // 4 - 1))
    mixed = jax.random.permutation(jax.random.fold_in(own, 3), count)
    donor, taker = mixed[0:count // 2 * 2:2], mixed[1:count // 2 * 2:2]
    margin = jnp.minimum(sizes[donor] - 1, reach - sizes[taker]) // 2
    margin = jnp.where((donor == sequence[0]) | (taker == sequence[0]) | (sizes[taker] == 0), 0, jnp.maximum(margin, 0))
    shifted = jax.random.randint(jax.random.fold_in(own, 4), (count // 2,), 0, 1 << 20) % (margin + 1)
    sizes = sizes.at[donor].add(-shifted).at[taker].add(shifted)
    items = jnp.searchsorted(jnp.cumsum(sizes), jnp.arange(rows * top), side="right").astype(jnp.int32)
    grid = items.reshape(top, rows).T
    grid = grid[jax.random.permutation(jax.random.fold_in(own, 1), rows)]
    rotation = jax.random.randint(jax.random.fold_in(own, 2), (rows, 1), 0, top)
    return jnp.take_along_axis(grid, (jnp.arange(top)[None, :] + rotation) % top, axis=1)


def portions_of(amount, total, limit, skew, full):
    loads = [(1 << 20) // math.isqrt(grade ** skew) + 1 for grade in range(1, amount + 1)]
    largest = limit if full else min(limit, max(-(-total // amount), total * loads[0] // sum(loads)))
    least = 1 if total - largest >= amount - 1 else 0
    holding, surplus = [largest] + [least] * (amount - 1), total - largest - least * (amount - 1)
    while surplus > 0:
        movable = [i for i in range(1, amount) if holding[i] < largest] or [i for i in range(1, amount) if holding[i] < limit]
        whole, left = sum([loads[i] for i in movable]), surplus
        for i in movable:
            extra = min(limit - holding[i], max(1, left * loads[i] // whole), surplus)
            holding[i] = holding[i] + extra
            surplus = surplus - extra
    return np.array(holding)


def gaussian(key, shape, deviation, limit, shards=(), kind=jnp.bfloat16):
    result = deviation * jax.random.normal(key, shape, jnp.float32)
    if shards:
        result = result * level_of(key, shape, shards, -0.22, 0.18)
    return jnp.clip(result, -limit, limit).astype(kind)


def setup_inputs(seed: int = 0) -> dict:
    seeds = jax.random.split(jax.random.key(seed), 8)
    saved_input = gaussian(seeds[0], (TOKENS, D), 1.0, 6.0, ((0, 16),))
    out_grad = gaussian(seeds[1], (TOKENS, D), 1.0, 6.0, ((0, 16),))
    routes_keys = jax.random.split(jax.random.fold_in(seeds[2], 1), TOKENS // TOK_DEV)
    routes_turns = jax.random.permutation(jax.random.fold_in(seeds[2], 3), TOKENS // TOK_DEV)
    routes = jax.vmap(lambda own, number: shared_out(jax.random.fold_in(seeds[2], 2), own, number, TOK_DEV, EXPERTS, TOPK, CAP, 2))(routes_keys, routes_turns).reshape((TOKENS, TOPK))
    gates = jnp.clip(jnp.exp(math.log(1.0) - 2.9996462 * jax.random.uniform(seeds[3], (TOKENS, TOPK), jnp.float32) ** level_of(seeds[3], (TOKENS, TOPK), ((0, 16),), -0.2, 0.2)), 0.049804688, 1.0).astype(jnp.bfloat16)
    gate_weight = gaussian(seeds[4], (EXPERTS, D, H), D ** -0.5, 0.09375, ((0, 16), (2, 8)))
    up_weight = gaussian(seeds[5], (EXPERTS, D, H), D ** -0.5, 0.09375, ((0, 16), (2, 8)))
    down_weight = gaussian(seeds[6], (EXPERTS, H, D), H ** -0.5, 0.125, ((0, 16), (1, 8)))
    return dict(saved_input=saved_input, out_grad=out_grad, routes=routes, gates=gates, gate_weight=gate_weight, up_weight=up_weight, down_weight=down_weight)


def slot_tables(routes):
    blocks = routes.reshape(N_LOCAL, TOK_DEV * TOPK)
    labels = jnp.arange(EXPERTS, dtype=jnp.int32)
    onehot = (blocks[:, :, None] == labels[None, None, :]).astype(jnp.int32)
    earlier = jnp.cumsum(onehot, axis=1) - onehot
    ranked = jnp.sum(earlier * onehot, axis=2)
    sources = jnp.arange(N_LOCAL, dtype=jnp.int32)[:, None]
    row_slot = (sources * CAP + ranked).reshape(-1).astype(jnp.int32)
    return routes.reshape(-1).astype(jnp.int32), row_slot


def expert_step(saved_ext, grad_ext, expert_item):
    gate_w, up_w, down_w, slot_index, weight = expert_item
    inputs = saved_ext[slot_index]
    upstream = grad_ext[slot_index]
    row_gate = weight[:, None]
    gate_pre = jnp.dot(inputs, gate_w, preferred_element_type=jnp.float32)
    up_pre = jnp.dot(inputs, up_w, preferred_element_type=jnp.float32)
    contract_feat = (((1,), (1,)), ((), ()))
    back_proj = lax.dot_general(upstream, down_w, contract_feat, preferred_element_type=jnp.float32)
    sigmoid = jax.nn.sigmoid(gate_pre)
    activated = gate_pre * sigmoid
    gate_term = jnp.sum(activated * up_pre * back_proj, axis=1)
    scaled_hidden = (row_gate * activated * up_pre).astype(jnp.bfloat16)
    hidden_grad = row_gate * back_proj
    grad_gate_pre = (hidden_grad * up_pre * sigmoid * (1.0 + gate_pre * (1.0 - sigmoid))).astype(jnp.bfloat16)
    grad_up_pre = (hidden_grad * activated).astype(jnp.bfloat16)
    contract_rows = (((0,), (0,)), ((), ()))
    grad_down = lax.dot_general(scaled_hidden, upstream, contract_rows, preferred_element_type=jnp.float32)
    grad_gate_w = lax.dot_general(inputs, grad_gate_pre, contract_rows, preferred_element_type=jnp.float32)
    grad_up_w = lax.dot_general(inputs, grad_up_pre, contract_rows, preferred_element_type=jnp.float32)
    partial_value = lax.dot_general(grad_gate_pre, gate_w, contract_feat, preferred_element_type=jnp.float32)
    partial_value = partial_value + lax.dot_general(grad_up_pre, up_w, contract_feat, preferred_element_type=jnp.float32)
    return gate_term, grad_gate_w, grad_up_w, grad_down, partial_value


def reference(saved_input, out_grad, routes, gates, gate_weight, up_weight, down_weight):
    slot_rows = N_LOCAL * CAP
    flat_ids, row_slot = slot_tables(routes)
    owner = jnp.arange(TOKENS * TOPK, dtype=jnp.int32) // TOPK
    table = jnp.full((EXPERTS, slot_rows), TOKENS, jnp.int32).at[flat_ids, row_slot].set(owner)
    weight_tab = jnp.zeros((EXPERTS, slot_rows), jnp.float32).at[flat_ids, row_slot].set(gates.reshape(-1).astype(jnp.float32))
    saved_ext = jnp.concatenate([saved_input, jnp.zeros((1, D), jnp.bfloat16)], axis=0)
    grad_ext = jnp.concatenate([out_grad, jnp.zeros((1, D), jnp.bfloat16)], axis=0)
    gate_terms, grad_gate_weight, grad_up_weight, grad_down_weight, partials = lax.map(
        lambda expert_item: expert_step(saved_ext, grad_ext, expert_item),
        (gate_weight, up_weight, down_weight, table, weight_tab))
    flat_rows = (flat_ids * slot_rows + row_slot).astype(jnp.int32)
    picked = jnp.take(partials.reshape(EXPERTS * slot_rows, D), flat_rows, axis=0)
    grad_input = jnp.sum(picked.reshape(TOKENS, TOPK, D), axis=1).astype(jnp.bfloat16)
    grad_gates = jnp.take(gate_terms.reshape(-1), flat_rows).reshape(TOKENS, TOPK)
    return grad_input, grad_gates, grad_gate_weight, grad_up_weight, grad_down_weight
```

```python
import functools

import jax
import jax.numpy as jnp
from jax import lax
from jax.experimental import pallas as pl
from jax.experimental.pallas import tpu as pltpu
from jax.sharding import PartitionSpec as P

MESH = pl.DeviceIdType.MESH
F32 = jnp.float32
BF16 = jnp.bfloat16
TOK = 256
FEAT = 3584
QUART = FEAT // 4
HID = 256
CAP = 64
ROWS = 16 * CAP
CHUNK = 4 * CAP
HALF = CHUNK // 2
WIN = 512
TILE = 512


def dot(a, b, dims):
    return lax.dot_general(a, b, (dims, ((), ())), preferred_element_type=F32)


def kernel(
    saved, ograd, routes, gates, gate_w, up_w, down_w,
    gin_o, gg_o, ggw_o, guw_o, gdw_o,
    tok, send, onehot, gsend, grecv, xy, w, wd, grad_pre, hidden, part,
    sib_in, z_in, ret, back, gt_send, gt_recv, gt_sib, gt_mine, gt_z,
    comb, comb_sib, opp_out, opp_in, dw_gu, dw_d,
    load_sem, disp_send, disp_recv, gate_send, gate_recv, fz_send, fz_recv, fs_send, fs_recv,
    sib_send, sib_recv, zr_send, zr_recv, ret_send, ret_recv, gts_send, gts_recv, gtx_send, gtx_recv,
    gtz_send, gtz_recv, cs_send, cs_recv, op_send, op_recv, out_sem,
):
    n, l = lax.axis_index("node"), lax.axis_index("local")
    z, c = lax.div(n, 2), lax.rem(n, 2)
    x, y = lax.div(l, 4), lax.rem(l, 4)
    other = 1 - c

    def plane(dx, dy):
        return (n, lax.rem(x + dx, 4) * 4 + lax.rem(y + dy, 4))

    def along_z(dz):
        return (lax.rem(z + dz, 4) * 2 + c, l)

    sibling = (z * 2 + other, l)

    def quarter(dz):
        return pl.ds(pl.multiple_of(lax.rem(z + dz, 4) * QUART, 128), QUART)

    def rows(start, size):
        return pl.ds(pl.multiple_of(start, size), size)

    def wait(ref, sem):
        pltpu.make_async_copy(ref, ref, sem).wait()

    def push(src, dst, send_sem, recv_sem, device):
        pltpu.make_async_remote_copy(
            src_ref=src, dst_ref=dst, send_sem=send_sem, recv_sem=recv_sem,
            device_id=device, device_id_type=MESH,
        ).start()

    def push_or_keep(here, src, dst, send_sem, recv_sem, device):
        @pl.when(here)
        def _():
            pltpu.make_async_copy(src, dst, recv_sem).start()

        @pl.when(jnp.logical_not(here))
        def _():
            push(src, dst, send_sem, recv_sem, device)

    barrier = pltpu.get_barrier_semaphore()
    for dx in range(4):
        for dy in range(4):
            if (dx, dy) != (0, 0):
                pl.semaphore_signal(barrier, inc=1, device_id=plane(dx, dy), device_id_type=MESH)
    for dz in (1, 2, 3):
        pl.semaphore_signal(barrier, inc=1, device_id=along_z(dz), device_id_type=MESH)
    pl.semaphore_signal(barrier, inc=1, device_id=sibling, device_id_type=MESH)

    for h in (0, 1):
        place = tok.at[:, pl.ds(h * QUART, QUART)]

        @pl.when(c == 0)
        def _():
            pltpu.make_async_copy(saved.at[:, quarter(h)], place, load_sem.at[0]).start()

        @pl.when(c == 1)
        def _():
            pltpu.make_async_copy(ograd.at[:, quarter(h)], place, load_sem.at[0]).start()

    pltpu.make_async_copy(gate_w, w.at[:, pl.ds(0, HID)], load_sem.at[1]).start()
    pltpu.make_async_copy(up_w, w.at[:, pl.ds(HID, HID)], load_sem.at[1]).start()
    pltpu.make_async_copy(down_w, wd, load_sem.at[2]).start()

    expert_lane = lax.broadcasted_iota(jnp.int32, (TOK, 128), 1)
    first = jnp.where(routes[:, 0:1] == expert_lane, 1.0, 0.0)
    second = jnp.where(routes[:, 1:2] == expert_lane, 1.0, 0.0)
    lower = jnp.where(
        lax.broadcasted_iota(jnp.int32, (TOK, TOK), 1) < lax.broadcasted_iota(jnp.int32, (TOK, TOK), 0), 1.0, 0.0
    ).astype(BF16)
    earlier = dot(lower, (first + second).astype(BF16), ((1,), (0,)))
    target0 = routes[:, 0:1].astype(F32) * CAP + jnp.sum(earlier * first, axis=1, keepdims=True)
    target1 = routes[:, 1:2].astype(F32) * CAP + jnp.sum(earlier * second, axis=1, keepdims=True)

    def slot_numbers(j):
        lane = lax.broadcasted_iota(jnp.int32, (1, CHUNK), 1)
        i = lax.div(lane, CAP)
        expert = lax.rem(x + i, 4) * 4 + lax.rem(y + i + j, 4)
        return (expert * CAP + lax.rem(lane, CAP)).astype(F32)

    for j in range(4):
        number = slot_numbers(j)
        hit0, hit1 = target0 == number, target1 == number
        onehot[:, j * CHUNK:(j + 1) * CHUNK] = jnp.where(hit0 | hit1, 1.0, 0.0).astype(BF16)
        weight = jnp.where(hit0, gates[:, 0:1].astype(F32), 0.0) + jnp.where(hit1, gates[:, 1:2].astype(F32), 0.0)
        gsend[:, j * CHUNK:(j + 1) * CHUNK] = jnp.broadcast_to(jnp.sum(weight, axis=0, keepdims=True), (8, CHUNK))

    wait(tok, load_sem.at[0])

    def pick(j):
        picked = dot(onehot[:, rows(j * CHUNK, CHUNK)], tok[...], ((0,), (0,)))
        send[rows(j * CHUNK, CHUNK), :] = picked.astype(BF16)

    def dispatch(j):
        for i in range(4):
            block = j * 4 + i
            device = plane(i, i + j)
            tile = gsend.at[:, rows(j * CHUNK + (i // 2) * 128, 128)]
            here = rows(block * CAP, CAP)
            copies = [(tile, grecv.at[block], gate_send, gate_recv)]
            for h in (0, 1):
                copies.append((
                    send.at[here, pl.ds(h * QUART, QUART)], xy.at[c, here, quarter(h)], disp_send, disp_recv.at[j, h],
                ))
            for src, dst, ssem, rsem in copies:
                if i == 0:
                    push_or_keep(j == 0, src, dst, ssem, rsem, device)
                else:
                    push(src, dst, ssem, rsem, device)

    pick(0)
    pl.semaphore_wait(barrier, 19)
    dispatch(0)

    @pl.loop(1, 4)
    def _(j):
        pick(j)
        dispatch(j)

    def forward(j):
        here = rows(j * CHUNK, CHUNK)
        for h, dz in ((0, 1), (1, 3)):
            block = xy.at[c, here, quarter(h)]
            wait(block, disp_recv.at[j, h])
            push(block, block, fz_send, fz_recv.at[j, h], along_z(dz))
            push(block, block, fs_send, fs_recv.at[j, h], sibling)

    def hand_over(j):
        here = rows(j * CHUNK, CHUNK)
        for h, dz in ((0, 3), (1, 2)):
            block = xy.at[c, here, quarter(dz)]
            wait(block, fz_recv.at[j, h])
            push(block, block, fs_send, fs_recv.at[j, 2 + h], sibling)

    def compute(j):
        here = rows(j * CHUNK, CHUNK)
        slot = lax.rem(j, 2)
        for h, dz in ((0, 0), (1, 1), (2, 3), (3, 2)):
            wait(xy.at[other, here, quarter(dz)], fs_recv.at[j, h])

        @pl.when(j == 0)
        def _():
            wait(grecv, gate_recv)
            wait(w, load_sem.at[1])
            wait(wd, load_sem.at[2])

        lane = lax.broadcasted_iota(jnp.int32, (CAP, 128), 1)
        row = lax.broadcasted_iota(jnp.int32, (CAP, 128), 0)
        cols = []
        for i in range(4):
            values = grecv[j * 4 + i][0:1, :]
            cols.append(jnp.sum(jnp.where(lane == row + (i % 2) * CAP, values, 0.0), axis=1, keepdims=True))
        gate = jnp.concatenate(cols, axis=0)
        pre = dot(xy[0, here, :], w[...], ((1,), (0,)))
        back_proj = dot(xy[1, here, :], wd[...], ((1,), (1,)))
        gate_pre, up_pre = pre[:, :HID], pre[:, HID:]
        sig = jax.nn.sigmoid(gate_pre)
        act = gate_pre * sig
        act_up = act * up_pre
        term = jnp.sum(act_up * back_proj, axis=1, keepdims=True)
        hidden[here, :] = (gate * act_up).astype(BF16)
        hidden_grad = gate * back_proj
        grad_pre[here, 0:HID] = (hidden_grad * up_pre * sig * (1.0 + gate_pre * (1.0 - sig))).astype(BF16)
        grad_pre[here, HID:2 * HID] = (hidden_grad * act).astype(BF16)

        eye = lax.broadcasted_iota(jnp.int32, (CHUNK, CHUNK), 0) == lax.broadcasted_iota(jnp.int32, (CHUNK, CHUNK), 1)
        term_row = jnp.sum(jnp.where(eye, term, 0.0), axis=0, keepdims=True)
        gt_send[:, here] = jnp.broadcast_to(term_row, (8, CHUNK))
        for i in range(4):
            device = plane(4 - i, 8 - i - j)
            tile = gt_send.at[:, rows(j * CHUNK + (i // 2) * 128, 128)]
            if i == 0:
                push_or_keep(j == 0, tile, gt_recv.at[j * 4 + i], gts_send, gts_recv, device)
            else:
                push(tile, gt_recv.at[j * 4 + i], gts_send, gts_recv, device)

        @pl.when(j >= 2)
        def _():
            wait(part.at[slot, pl.ds(0, HALF)], sib_send.at[slot])
            wait(part.at[slot, pl.ds(0, HALF), pl.ds(0, 2 * QUART)], zr_send.at[slot])

        @pl.loop(0, FEAT // TILE)
        def _(t):
            cut = rows(t * TILE, TILE)
            part[slot, :, cut] = dot(grad_pre[here, :], w[cut, :], ((1,), (1,))).astype(BF16)

        push(
            part.at[slot, rows(other * HALF, HALF)], sib_in.at[rows(j * HALF, HALF)],
            sib_send.at[slot], sib_recv.at[j], sibling,
        )

    def sum_cores(j):
        slot = lax.rem(j, 2)
        mine, here = rows(c * HALF, HALF), rows(j * HALF, HALF)
        wait(sib_in.at[here], sib_recv.at[j])

        @pl.loop(0, FEAT // TILE)
        def _(t):
            cut = rows(t * TILE, TILE)
            part[slot, mine, cut] = (part[slot, mine, cut].astype(F32) + sib_in[here, cut].astype(F32)).astype(BF16)

        for h, dz in ((0, 1), (1, 3)):
            push(part.at[slot, mine, quarter(dz)], z_in.at[h, here], zr_send.at[slot], zr_recv.at[j, h], along_z(dz))
        ret[0, here, :] = part[slot, mine, quarter(0)]
        ret[1, here, :] = part[slot, mine, quarter(2)]
        send_back(j, 1)

    def send_back(j, s):
        for ii in (0, 1):
            i = 2 * c + ii
            here = rows(j * HALF + ii * CAP, CAP)
            device = plane(4 - i, 8 - i - j)
            args = (ret.at[s, here], back.at[s, here], ret_send, ret_recv.at[s], device)
            if ii == 0:
                push_or_keep((j == 0) & (c == 0), *args)
            else:
                push(*args)

    def sum_planes(j):
        here = rows(j * HALF, HALF)
        for h in (0, 1):
            wait(z_in.at[h, here], zr_recv.at[j, h])
        ret[0, here, :] = (
            ret[0, here, :].astype(F32) + z_in[0, here, :].astype(F32) + z_in[1, here, :].astype(F32)
        ).astype(BF16)
        send_back(j, 0)

    def weight_grads(j):
        here = rows(j * CHUNK, CHUNK)
        turned = hidden[here, :].T

        @pl.loop(0, FEAT // TILE)
        def _(t):
            cut = rows(t * TILE, TILE)
            gu = dot(xy[0, here, cut], grad_pre[here, :], ((0,), (0,)))
            down = dot(turned, xy[1, here, cut], ((1,), (0,)))

            @pl.when(j == 0)
            def _():
                dw_gu[cut, :] = gu
                dw_d[:, cut] = down

            @pl.when(j > 0)
            def _():
                dw_gu[cut, :] += gu
                dw_d[:, cut] += down

    forward(0)

    @pl.loop(0, 4)
    def _(j):
        @pl.when(j < 3)
        def _():
            forward(j + 1)

        hand_over(j)
        compute(j)
        sum_cores(j)

        @pl.when(j > 0)
        def _():
            sum_planes(j - 1)

        weight_grads(j)

    outs = (
        (dw_gu.at[:, pl.ds(0, HID)], ggw_o), (dw_gu.at[:, pl.ds(HID, HID)], guw_o), (dw_d, gdw_o),
    )
    for i, (src, dst) in enumerate(outs):
        pltpu.make_async_copy(src, dst, out_sem.at[i]).start()
    sum_planes(3)

    wait(gt_recv, gts_recv)
    low = lax.broadcasted_iota(jnp.int32, (8, 128), 1) < CAP
    for m in range(8):
        gt_mine[:, m * 128:(m + 1) * 128] = jnp.where(low, gt_recv[2 * m], gt_recv[2 * m + 1])
    push(gt_mine, gt_sib, gtx_send, gtx_recv, sibling)

    def combine(s):
        total = jnp.zeros((TOK, QUART), F32)
        for j in range(4):
            hits = onehot[:, rows(j * CHUNK + c * HALF, HALF)]
            total += dot(hits, back[s, j * HALF:(j + 1) * HALF, :], ((1,), (0,)))
        comb[s, :, :] = total

    def window(core):
        return pl.ds(pl.multiple_of(core * (QUART - WIN), 128), WIN)

    wait(back.at[1], ret_recv.at[1])
    combine(1)
    push(comb.at[1, :, window(other)], comb_sib.at[1], cs_send.at[1], cs_recv.at[1], sibling)

    wait(gt_sib, gtx_recv)
    gt_z[z] = gt_mine[...] + gt_sib[...]
    for dz in (1, 2, 3):
        push(gt_z.at[z], gt_z.at[z], gtz_send.at[dz], gtz_recv.at[dz], along_z(dz))

    wait(comb_sib.at[1], cs_recv.at[1])
    opp_out[...] = (comb[1, :, window(c)] + comb_sib[1]).astype(BF16)
    push(opp_out, opp_in, op_send, op_recv, along_z(2))

    wait(back.at[0], ret_recv.at[0])
    combine(0)
    push(comb.at[0, :, window(other)], comb_sib.at[0], cs_send.at[0], cs_recv.at[0], sibling)

    for dz in (1, 2, 3):
        wait(gt_z.at[lax.rem(z + 4 - dz, 4)], gtz_recv.at[dz])
    total_row = (gt_z[0] + gt_z[1] + gt_z[2] + gt_z[3])[0:1, :]
    sum0, sum1 = jnp.zeros((TOK, 1), F32), jnp.zeros((TOK, 1), F32)
    for j in range(4):
        number = slot_numbers(j)
        term = total_row[:, j * CHUNK:(j + 1) * CHUNK]
        sum0 += jnp.sum(jnp.where(target0 == number, term, 0.0), axis=1, keepdims=True)
        sum1 += jnp.sum(jnp.where(target1 == number, term, 0.0), axis=1, keepdims=True)
    gg_o[:, 0:1] = sum0
    gg_o[:, 1:2] = sum1

    wait(comb_sib.at[0], cs_recv.at[0])
    wait(opp_in, op_recv)
    result = (comb[0, :, window(c)] + comb_sib[0] + opp_in[...].astype(F32)).astype(BF16)

    @pl.when(c == 0)
    def _():
        gin_o[...] = result[:, 0:QUART // 2]

    @pl.when(c == 1)
    def _():
        gin_o[...] = result[:, WIN - QUART // 2:WIN]

    for i, (src, dst) in enumerate(outs):
        pltpu.make_async_copy(src, dst, out_sem.at[i]).wait()
    wait(send.at[pl.ds(CAP, ROWS - CAP)], disp_send)
    wait(grecv.at[pl.ds(1, 15)], gate_send)
    wait(gt_recv.at[pl.ds(1, 15)], gts_send)
    wait(send, fz_send)
    wait(xy.at[c], fs_send)
    for slot in (0, 1):
        wait(part.at[slot, pl.ds(0, HALF)], sib_send.at[slot])
        wait(part.at[slot, pl.ds(0, HALF), pl.ds(0, 2 * QUART)], zr_send.at[slot])

    @pl.when(c == 0)
    def _():
        wait(ret.at[0, pl.ds(CAP, 512 - CAP)], ret_send)
        wait(ret.at[1, pl.ds(CAP, 512 - CAP)], ret_send)

    @pl.when(c == 1)
    def _():
        wait(ret.at[0], ret_send)
        wait(ret.at[1], ret_send)

    wait(gt_mine, gtx_send)
    for dz in (1, 2, 3):
        wait(gt_z.at[z], gtz_send.at[dz])
    for s in (0, 1):
        wait(comb_sib.at[s], cs_send.at[s])
    wait(opp_out, op_send)


def on_device(saved_input, out_grad, routes, gates, gate_weight, up_weight, down_weight):
    anywhere = pl.BlockSpec(memory_space=pl.ANY)
    vmem = pl.BlockSpec(memory_space=pltpu.VMEM)
    dma = pltpu.SemaphoreType.DMA
    scratch = [
        pltpu.VMEM((TOK, 2 * QUART), BF16),
        pltpu.VMEM((ROWS, 2 * QUART), BF16),
        pltpu.VMEM((TOK, ROWS), BF16),
        pltpu.VMEM((8, ROWS), F32),
        pltpu.VMEM((16, 8, 128), F32),
        pltpu.VMEM((2, ROWS, FEAT), BF16),
        pltpu.VMEM((FEAT, 2 * HID), BF16),
        pltpu.VMEM((HID, FEAT), BF16),
        pltpu.VMEM((ROWS, 2 * HID), BF16),
        pltpu.VMEM((ROWS, HID), BF16),
        pltpu.VMEM((2, CHUNK, FEAT), BF16),
        pltpu.VMEM((ROWS // 2, FEAT), BF16),
        pltpu.VMEM((2, ROWS // 2, QUART), BF16),
        pltpu.VMEM((2, ROWS // 2, QUART), BF16),
        pltpu.VMEM((2, ROWS // 2, QUART), BF16),
        pltpu.VMEM((8, ROWS), F32),
        pltpu.VMEM((16, 8, 128), F32),
        pltpu.VMEM((8, ROWS), F32),
        pltpu.VMEM((8, ROWS), F32),
        pltpu.VMEM((4, 8, ROWS), F32),
        pltpu.VMEM((2, TOK, QUART), F32),
        pltpu.VMEM((2, TOK, WIN), F32),
        pltpu.VMEM((TOK, WIN), BF16),
        pltpu.VMEM((TOK, WIN), BF16),
        pltpu.VMEM((FEAT, 2 * HID), F32),
        pltpu.VMEM((HID, FEAT), F32),
        dma((3,)),
        dma(()), dma((4, 2)),
        dma(()), dma(()),
        dma(()), dma((4, 2)),
        dma(()), dma((4, 4)),
        dma((2,)), dma((4,)),
        dma((2,)), dma((4, 2)),
        dma(()), dma((2,)),
        dma(()), dma(()),
        dma(()), dma(()),
        dma((4,)), dma((4,)),
        dma((2,)), dma((2,)),
        dma(()), dma(()),
        dma((3,)),
    ]
    gin, gg, ggw, guw, gdw = pl.pallas_call(
        kernel,
        out_shape=(
            jax.ShapeDtypeStruct((TOK, QUART // 2), BF16),
            jax.ShapeDtypeStruct((TOK, 2), F32),
            jax.ShapeDtypeStruct((FEAT, HID), F32),
            jax.ShapeDtypeStruct((FEAT, HID), F32),
            jax.ShapeDtypeStruct((HID, FEAT), F32),
        ),
        in_specs=[anywhere, anywhere, vmem, vmem, anywhere, anywhere, anywhere],
        out_specs=(vmem, vmem, anywhere, anywhere, anywhere),
        scratch_shapes=scratch,
        compiler_params=pltpu.CompilerParams(
            collective_id=0, has_side_effects=True, vmem_limit_bytes=62 * 2**20
        ),
        cost_estimate=pl.CostEstimate(flops=15 * 10**9, bytes_accessed=20 * 10**6, transcendentals=10**6),
    )(saved_input, out_grad, routes, gates, gate_weight[0], up_weight[0], down_weight[0])
    return gin, gg, ggw[None], guw[None], gdw[None]


def solution(mesh):
    placed = (
        P("local", None),
        P("local", None),
        P("local", None),
        P("local", None),
        P("local", None, "node"),
        P("local", None, "node"),
        P("local", "node", None),
    )
    return jax.shard_map(
        on_device,
        mesh=mesh,
        in_specs=placed,
        out_specs=(
            P("local", "node"),
            P("local", None),
            P("local", None, "node"),
            P("local", None, "node"),
            P("local", "node", None),
        ),
        check_vma=False,
    )
```

```python
import functools

import jax
import jax.numpy as jnp
from jax import lax
from jax.experimental import pallas as pl
from jax.experimental.pallas import tpu as pltpu
from jax.sharding import PartitionSpec as P

MESH = pl.DeviceIdType.MESH
F32 = jnp.float32
BF16 = jnp.bfloat16
TOK = 256
FEAT = 3584
QUART = FEAT // 4
HID = 256
CAP = 64
ROWS = 16 * CAP
CHUNK = 4 * CAP
HALF = CHUNK // 2
WIN = 512
TILE = 512

OFFSETS = (
    ((0, 1), (0, 3), (1, 0), (3, 0)),
    ((0, 0), (2, 2), (2, 0), (0, 2)),
    ((1, 1), (3, 3), (1, 3), (3, 1)),
    ((1, 2), (3, 2), (2, 1), (2, 3)),
)
SELF = (1, 0)


def dot(a, b, dims):
    return lax.dot_general(a, b, (dims, ((), ())), preferred_element_type=F32)


def eye(size):
    return lax.broadcasted_iota(jnp.int32, (size, size), 0) == lax.broadcasted_iota(jnp.int32, (size, size), 1)


def column(row):
    return jnp.sum(jnp.where(eye(TOK), row, 0.0), axis=1, keepdims=True)


def as_row(col):
    return jnp.sum(jnp.where(eye(TOK), col, 0.0), axis=0, keepdims=True)


def kernel(
    saved, ograd, routes, gates, gate_w, up_w, down_w,
    gin_o, gg_o, ggw_o, guw_o, gdw_o,
    tok, send, onehot, gsend, grecv, xy, w, wd, grad_pre, hidden, part,
    sib_in, z_in, ret, back, gt_send, gt_recv, gt_sib, gt_mine, gt_z,
    comb, comb_sib, opp_out, opp_in, dw_gu, dw_d, stage_gu, stage_d,
    load_sem, disp_send, disp_recv, gate_send, gate_recv, fz_send, fz_recv, fs_send, fs_recv,
    sib_send, sib_recv, zr_send, zr_recv, ret_send, ret_recv, gts_send, gts_recv, gtx_send, gtx_recv,
    gtz_send, gtz_recv, cs_send, cs_recv, op_send, op_recv, out_sem,
):
    n, l = lax.axis_index("node"), lax.axis_index("local")
    z, c = lax.div(n, 2), lax.rem(n, 2)
    x, y = lax.div(l, 4), lax.rem(l, 4)
    other = 1 - c

    def plane(dx, dy):
        return (n, lax.rem(x + dx, 4) * 4 + lax.rem(y + dy, 4))

    def along_z(dz):
        return (lax.rem(z + dz, 4) * 2 + c, l)

    sibling = (z * 2 + other, l)

    def quarter(dz):
        return pl.ds(pl.multiple_of(lax.rem(z + dz, 4) * QUART, 128), QUART)

    def rows(start, size):
        return pl.ds(pl.multiple_of(start, size), size)

    def wait(ref, sem):
        pltpu.make_async_copy(ref, ref, sem).wait()

    def push(src, dst, send_sem, recv_sem, device):
        pltpu.make_async_remote_copy(
            src_ref=src, dst_ref=dst, send_sem=send_sem, recv_sem=recv_sem,
            device_id=device, device_id_type=MESH,
        ).start()

    barrier = pltpu.get_barrier_semaphore()
    for dx in range(4):
        for dy in range(4):
            if (dx, dy) != (0, 0):
                pl.semaphore_signal(barrier, inc=1, device_id=plane(dx, dy), device_id_type=MESH)
    for dz in (1, 2, 3):
        pl.semaphore_signal(barrier, inc=1, device_id=along_z(dz), device_id_type=MESH)
    pl.semaphore_signal(barrier, inc=1, device_id=sibling, device_id_type=MESH)

    for h in (0, 1):
        place = tok.at[:, pl.ds(h * QUART, QUART)]

        @pl.when(c == 0)
        def _():
            pltpu.make_async_copy(saved.at[:, quarter(h)], place, load_sem.at[0]).start()

        @pl.when(c == 1)
        def _():
            pltpu.make_async_copy(ograd.at[:, quarter(h)], place, load_sem.at[0]).start()

    pltpu.make_async_copy(gate_w, w.at[:, pl.ds(0, HID)], load_sem.at[1]).start()
    pltpu.make_async_copy(up_w, w.at[:, pl.ds(HID, HID)], load_sem.at[1]).start()
    pltpu.make_async_copy(down_w, wd, load_sem.at[2]).start()

    route0, route1 = column(routes[0:1, :].astype(F32)), column(routes[1:2, :].astype(F32))
    gate0, gate1 = column(gates[0:1, :].astype(F32)), column(gates[1:2, :].astype(F32))
    expert_lane = lax.broadcasted_iota(jnp.int32, (TOK, 128), 1).astype(F32)
    first = jnp.where(route0 == expert_lane, 1.0, 0.0)
    second = jnp.where(route1 == expert_lane, 1.0, 0.0)
    lower = jnp.where(
        lax.broadcasted_iota(jnp.int32, (TOK, TOK), 1) < lax.broadcasted_iota(jnp.int32, (TOK, TOK), 0), 1.0, 0.0
    ).astype(BF16)
    earlier = dot(lower, (first + second).astype(BF16), ((1,), (0,)))
    target0 = route0 * CAP + jnp.sum(earlier * first, axis=1, keepdims=True)
    target1 = route1 * CAP + jnp.sum(earlier * second, axis=1, keepdims=True)

    def slot_numbers(j):
        lane = lax.broadcasted_iota(jnp.int32, (1, CHUNK), 1)
        which, number = lax.div(lane, CAP), lax.rem(lane, CAP)
        for i, (dx, dy) in enumerate(OFFSETS[j]):
            expert = lax.rem(x + dx, 4) * 4 + lax.rem(y + dy, 4)
            number = number + jnp.where(which == i, expert * CAP, 0)
        return number.astype(F32)

    def mark(j):
        number = slot_numbers(j)
        hit0, hit1 = target0 == number, target1 == number
        onehot[:, j * CHUNK:(j + 1) * CHUNK] = jnp.where(hit0 | hit1, 1.0, 0.0).astype(BF16)
        weight = jnp.where(hit0, gate0, 0.0) + jnp.where(hit1, gate1, 0.0)
        gsend[:, j * CHUNK:(j + 1) * CHUNK] = jnp.broadcast_to(jnp.sum(weight, axis=0, keepdims=True), (8, CHUNK))

    def pick(j):
        picked = dot(onehot[:, j * CHUNK:(j + 1) * CHUNK], tok[...], ((0,), (0,)))
        send[j * CHUNK:(j + 1) * CHUNK, :] = picked.astype(BF16)

    def send_gates(j):
        for i, (dx, dy) in enumerate(OFFSETS[j]):
            tile = gsend.at[:, pl.ds(j * CHUNK + (i // 2) * 128, 128)]
            if (j, i) == SELF:
                pltpu.make_async_copy(tile, grecv.at[j * 4 + i], gate_recv).start()
            else:
                push(tile, grecv.at[j * 4 + i], gate_send, gate_recv, plane(dx, dy))

    def dispatch(j, h, p=None):
        for i, (dx, dy) in enumerate(OFFSETS[j]):
            if p is not None and i // 2 != p:
                continue
            here = pl.ds((j * 4 + i) * CAP, CAP)
            src, dst = send.at[here, pl.ds(h * QUART, QUART)], xy.at[c, here, quarter(h)]
            rsem = disp_recv.at[j + (p or 0), h]
            if (j, i) == SELF:
                pltpu.make_async_copy(src, dst, rsem).start()
            else:
                push(src, dst, disp_send, rsem, plane(dx, dy))

    def forward(j, h, p=None):
        here = pl.ds(j * CHUNK, CHUNK) if p is None else pl.ds(j * CHUNK + p * HALF, HALF)
        block = xy.at[c, here, quarter(h)]
        wait(block, disp_recv.at[j + (p or 0), h])
        push(block, block, fz_send, fz_recv.at[j, h], along_z((1, 3)[h]))
        push(block, block, fs_send, fs_recv.at[j, h], sibling)

    def hand_over(j):
        here = pl.ds(j * CHUNK, CHUNK)
        for h, dz in ((0, 3), (1, 2)):
            block = xy.at[c, here, quarter(dz)]
            wait(block, fz_recv.at[j, h])
            push(block, block, fs_send, fs_recv.at[j, 2 + h], sibling)

    def compute(j):
        here = pl.ds(j * CHUNK, CHUNK)
        slot = j % 2
        for h, dz in ((0, 0), (1, 1), (2, 3), (3, 2)):
            wait(xy.at[other, here, quarter(dz)], fs_recv.at[j, h])
        lane = lax.broadcasted_iota(jnp.int32, (CAP, 128), 1)
        row = lax.broadcasted_iota(jnp.int32, (CAP, 128), 0)
        cols = []
        for i in range(4):
            values = grecv[j * 4 + i][0:1, :]
            cols.append(jnp.sum(jnp.where(lane == row + (i % 2) * CAP, values, 0.0), axis=1, keepdims=True))
        gate = jnp.concatenate(cols, axis=0)
        pre = dot(xy[0, here, :], w[...], ((1,), (0,)))
        back_proj = dot(xy[1, here, :], wd[...], ((1,), (1,)))
        gate_pre, up_pre = pre[:, :HID], pre[:, HID:]
        sig = jax.nn.sigmoid(gate_pre)
        act = gate_pre * sig
        act_up = act * up_pre
        term = jnp.sum(act_up * back_proj, axis=1, keepdims=True)
        hidden[here, :] = (gate * act_up).astype(BF16)
        hidden_grad = gate * back_proj
        grad_pre[here, 0:HID] = (hidden_grad * up_pre * sig * (1.0 + gate_pre * (1.0 - sig))).astype(BF16)
        grad_pre[here, HID:2 * HID] = (hidden_grad * act).astype(BF16)
        gt_send[:, here] = jnp.broadcast_to(as_row(term), (8, CHUNK))

        if j >= 2:
            wait(part.at[slot, pl.ds(0, HALF)], sib_send.at[slot])
            wait(part.at[slot, pl.ds(0, HALF), pl.ds(0, 2 * QUART)], zr_send.at[slot])
        for dz in (1, 3, 2, 0):
            cut = quarter(dz)
            part[slot, :, cut] = dot(grad_pre[here, :], w[cut, :], ((1,), (1,))).astype(BF16)
            push(
                part.at[slot, rows(other * HALF, HALF), cut], sib_in.at[pl.ds(j * HALF, HALF), cut],
                sib_send.at[slot], sib_recv.at[j, dz], sibling,
            )
        for i, (dx, dy) in enumerate(OFFSETS[j]):
            tile = gt_send.at[:, pl.ds(j * CHUNK + (i // 2) * 128, 128)]
            if (j, i) == SELF:
                pltpu.make_async_copy(tile, gt_recv.at[j * 4 + i], gts_recv).start()
            else:
                push(tile, gt_recv.at[j * 4 + i], gts_send, gts_recv, plane(4 - dx, 4 - dy))

    def sum_cores(j):
        slot = j % 2
        mine, here = rows(c * HALF, HALF), pl.ds(j * HALF, HALF)
        for h, dz in ((0, 1), (1, 3)):
            cut = quarter(dz)
            wait(sib_in.at[here, cut], sib_recv.at[j, dz])
            part[slot, mine, cut] = (part[slot, mine, cut].astype(F32) + sib_in[here, cut].astype(F32)).astype(BF16)
            push(part.at[slot, mine, cut], z_in.at[h, here], zr_send.at[slot], zr_recv.at[j, h], along_z(dz))
        cut = quarter(2)
        wait(sib_in.at[here, cut], sib_recv.at[j, 2])
        ret[1, here, :] = (part[slot, mine, cut].astype(F32) + sib_in[here, cut].astype(F32)).astype(BF16)
        send_back(j, 1)

    def send_back(j, s):
        for ii in (0, 1):
            (dx0, dy0), (dx1, dy1) = OFFSETS[j][ii], OFFSETS[j][2 + ii]
            device = plane(4 - dx0 + c * (dx0 - dx1), 4 - dy0 + c * (dy0 - dy1))
            here = pl.ds(j * HALF + ii * CAP, CAP)
            src, dst, rsem = ret.at[s, here], back.at[s, here], ret_recv.at[s, j]
            if (j, ii) == SELF:
                @pl.when(c == 0)
                def _():
                    pltpu.make_async_copy(src, dst, rsem).start()

                @pl.when(c == 1)
                def _():
                    push(src, dst, ret_send, rsem, device)
            else:
                push(src, dst, ret_send, rsem, device)

    def sum_planes(j):
        slot = j % 2
        mine, here = rows(c * HALF, HALF), pl.ds(j * HALF, HALF)
        cut = quarter(0)
        wait(sib_in.at[here, cut], sib_recv.at[j, 0])
        total = part[slot, mine, cut].astype(F32) + sib_in[here, cut].astype(F32)
        for h in (0, 1):
            wait(z_in.at[h, here], zr_recv.at[j, h])
        ret[0, here, :] = (total + z_in[0, here, :].astype(F32) + z_in[1, here, :].astype(F32)).astype(BF16)
        send_back(j, 0)

    def weight_grads(j):
        here = pl.ds(j * CHUNK, CHUNK)
        turned = hidden[here, :].T

        @pl.loop(0, FEAT // TILE)
        def _(t):
            cut = rows(t * TILE, TILE)
            gu = dot(xy[0, here, cut], grad_pre[here, :], ((0,), (0,)))
            down = dot(turned, xy[1, here, cut], ((1,), (0,)))
            if j == 0:
                dw_gu[cut, :] = gu
                dw_d[:, cut] = down
            elif j < 3:
                dw_gu[cut, :] += gu
                dw_d[:, cut] += down
            else:
                stage_gu[cut, :] = (dw_gu[cut, :] + gu).astype(BF16)
                stage_d[:, cut] = (dw_d[:, cut] + down).astype(BF16)

    def combine(s, j):
        here = pl.ds(j * HALF, HALF)
        wait(back.at[s, here], ret_recv.at[s, j])
        total = dot(onehot[:, rows(j * CHUNK + c * HALF, HALF)], back[s, here, :], ((1,), (0,)))
        if j == 0:
            comb[s, :, :] = total
        else:
            comb[s, :, :] += total

    def window(core):
        return pl.ds(pl.multiple_of(core * (QUART - WIN), 128), WIN)

    def trade(s):
        push(comb.at[s, :, window(other)], comb_sib.at[s], cs_send.at[s], cs_recv.at[s], sibling)

    for j in range(4):
        mark(j)
    wait(tok, load_sem.at[0])
    pick(0)
    pl.semaphore_wait(barrier, 19)
    for j in range(4):
        send_gates(j)
    dispatch(0, 0)
    dispatch(0, 1)
    pick(1)
    pick(2)
    pick(3)

    forward(0, 0)
    dispatch(1, 0)
    forward(0, 1)
    dispatch(1, 1)
    forward(1, 0)
    dispatch(2, 0)
    hand_over(0)
    wait(grecv, gate_recv)
    wait(w, load_sem.at[1])
    wait(wd, load_sem.at[2])
    forward(1, 1)
    dispatch(2, 1)
    compute(0)
    forward(2, 0)
    dispatch(3, 0, 0)
    dispatch(3, 1, 0)
    sum_cores(0)
    forward(2, 1)
    hand_over(1)
    compute(1)
    forward(3, 0, 0)
    dispatch(3, 0, 1)
    sum_cores(1)
    forward(3, 1, 0)
    dispatch(3, 1, 1)
    sum_planes(0)
    hand_over(2)
    forward(3, 0, 1)
    compute(2)
    forward(3, 1, 1)
    sum_cores(2)
    sum_planes(1)
    weight_grads(0)
    hand_over(3)
    compute(3)
    sum_cores(3)
    sum_planes(2)
    weight_grads(1)
    for s in (0, 1):
        combine(s, 0)
        combine(s, 1)
    combine(1, 2)
    weight_grads(2)
    wait(gt_recv, gts_recv)
    low = lax.broadcasted_iota(jnp.int32, (8, 128), 1) < CAP
    for m in range(8):
        gt_mine[:, m * 128:(m + 1) * 128] = jnp.where(low, gt_recv[2 * m], gt_recv[2 * m + 1])
    push(gt_mine, gt_sib, gtx_send, gtx_recv, sibling)
    combine(1, 3)
    trade(1)
    sum_planes(3)
    wait(gt_sib, gtx_recv)
    gt_z[z] = gt_mine[...] + gt_sib[...]
    for dz in (1, 2, 3):
        push(gt_z.at[z], gt_z.at[z], gtz_send.at[dz], gtz_recv.at[dz], along_z(dz))
    weight_grads(3)
    outs = (
        (stage_gu.at[:, pl.ds(0, HID)], ggw_o), (stage_gu.at[:, pl.ds(HID, HID)], guw_o), (stage_d, gdw_o),
    )
    for i, (src, dst) in enumerate(outs):
        pltpu.make_async_copy(src, dst, out_sem.at[i]).start()
    wait(comb_sib.at[1], cs_recv.at[1])
    opp_out[...] = (comb[1, :, window(c)] + comb_sib[1]).astype(BF16)
    push(opp_out, opp_in, op_send, op_recv, along_z(2))
    combine(0, 2)
    combine(0, 3)
    trade(0)

    for dz in (1, 2, 3):
        wait(gt_z.at[lax.rem(z + 4 - dz, 4)], gtz_recv.at[dz])
    total_row = (gt_z[0] + gt_z[1] + gt_z[2] + gt_z[3])[0:1, :]
    sum0, sum1 = jnp.zeros((TOK, 1), F32), jnp.zeros((TOK, 1), F32)
    for j in range(4):
        number = slot_numbers(j)
        term = total_row[:, j * CHUNK:(j + 1) * CHUNK]
        sum0 += jnp.sum(jnp.where(target0 == number, term, 0.0), axis=1, keepdims=True)
        sum1 += jnp.sum(jnp.where(target1 == number, term, 0.0), axis=1, keepdims=True)
    gg_o[0:1, :] = as_row(sum0)
    gg_o[1:2, :] = as_row(sum1)

    wait(comb_sib.at[0], cs_recv.at[0])
    wait(opp_in, op_recv)
    result = (comb[0, :, window(c)] + comb_sib[0] + opp_in[...].astype(F32)).T.astype(BF16)

    @pl.when(c == 0)
    def _():
        gin_o[...] = result[0:QUART // 2, :]

    @pl.when(c == 1)
    def _():
        gin_o[...] = result[WIN - QUART // 2:WIN, :]

    for i, (src, dst) in enumerate(outs):
        pltpu.make_async_copy(src, dst, out_sem.at[i]).wait()
    wait(send.at[pl.ds(CAP, ROWS - CAP)], disp_send)
    wait(grecv.at[pl.ds(1, 15)], gate_send)
    wait(gt_recv.at[pl.ds(1, 15)], gts_send)
    wait(send, fz_send)
    wait(xy.at[c], fs_send)
    for slot in (0, 1):
        wait(part.at[slot, pl.ds(0, HALF)], sib_send.at[slot])
        wait(part.at[slot, pl.ds(0, HALF), pl.ds(0, 2 * QUART)], zr_send.at[slot])

    @pl.when(c == 0)
    def _():
        wait(ret.at[0, pl.ds(CAP, 512 - CAP)], ret_send)
        wait(ret.at[1, pl.ds(CAP, 512 - CAP)], ret_send)

    @pl.when(c == 1)
    def _():
        wait(ret.at[0], ret_send)
        wait(ret.at[1], ret_send)

    wait(gt_mine, gtx_send)
    for dz in (1, 2, 3):
        wait(gt_z.at[z], gtz_send.at[dz])
    for s in (0, 1):
        wait(comb_sib.at[s], cs_send.at[s])
    wait(opp_out, op_send)


def on_device(saved_input, out_grad, routes, gates, gate_weight, up_weight, down_weight):
    anywhere = pl.BlockSpec(memory_space=pl.ANY)
    vmem = pl.BlockSpec(memory_space=pltpu.VMEM)
    dma = pltpu.SemaphoreType.DMA
    scratch = [
        pltpu.VMEM((TOK, 2 * QUART), BF16),
        pltpu.VMEM((ROWS, 2 * QUART), BF16),
        pltpu.VMEM((TOK, ROWS), BF16),
        pltpu.VMEM((8, ROWS), F32),
        pltpu.VMEM((16, 8, 128), F32),
        pltpu.VMEM((2, ROWS, FEAT), BF16),
        pltpu.VMEM((FEAT, 2 * HID), BF16),
        pltpu.VMEM((HID, FEAT), BF16),
        pltpu.VMEM((ROWS, 2 * HID), BF16),
        pltpu.VMEM((ROWS, HID), BF16),
        pltpu.VMEM((2, CHUNK, FEAT), BF16),
        pltpu.VMEM((ROWS // 2, FEAT), BF16),
        pltpu.VMEM((2, ROWS // 2, QUART), BF16),
        pltpu.VMEM((2, ROWS // 2, QUART), BF16),
        pltpu.VMEM((2, ROWS // 2, QUART), BF16),
        pltpu.VMEM((8, ROWS), F32),
        pltpu.VMEM((16, 8, 128), F32),
        pltpu.VMEM((8, ROWS), F32),
        pltpu.VMEM((8, ROWS), F32),
        pltpu.VMEM((4, 8, ROWS), F32),
        pltpu.VMEM((2, TOK, QUART), F32),
        pltpu.VMEM((2, TOK, WIN), F32),
        pltpu.VMEM((TOK, WIN), BF16),
        pltpu.VMEM((TOK, WIN), BF16),
        pltpu.VMEM((FEAT, 2 * HID), F32),
        pltpu.VMEM((HID, FEAT), F32),
        pltpu.VMEM((FEAT, 2 * HID), BF16),
        pltpu.VMEM((HID, FEAT), BF16),
        dma((3,)),
        dma(()), dma((5, 2)),
        dma(()), dma(()),
        dma(()), dma((4, 2)),
        dma(()), dma((4, 4)),
        dma((2,)), dma((4, 4)),
        dma((2,)), dma((4, 2)),
        dma(()), dma((2, 4)),
        dma(()), dma(()),
        dma(()), dma(()),
        dma((4,)), dma((4,)),
        dma((2,)), dma((2,)),
        dma(()), dma(()),
        dma((3,)),
    ]
    gin, gg, ggw, guw, gdw = pl.pallas_call(
        kernel,
        out_shape=(
            jax.ShapeDtypeStruct((QUART // 2, TOK), BF16),
            jax.ShapeDtypeStruct((2, TOK), F32),
            jax.ShapeDtypeStruct((FEAT, HID), BF16),
            jax.ShapeDtypeStruct((FEAT, HID), BF16),
            jax.ShapeDtypeStruct((HID, FEAT), BF16),
        ),
        in_specs=[anywhere, anywhere, vmem, vmem, anywhere, anywhere, anywhere],
        out_specs=(vmem, vmem, anywhere, anywhere, anywhere),
        scratch_shapes=scratch,
        compiler_params=pltpu.CompilerParams(
            collective_id=0, has_side_effects=True, vmem_limit_bytes=62 * 2**20
        ),
        cost_estimate=pl.CostEstimate(flops=15 * 10**9, bytes_accessed=20 * 10**6, transcendentals=10**6),
    )(saved_input, out_grad, routes.T, gates.T, gate_weight[0], up_weight[0], down_weight[0])
    ggw, guw, gdw = (grad.astype(F32)[None] for grad in (ggw, guw, gdw))
    return gin.T, gg.T, ggw, guw, gdw


def solution(mesh):
    placed = (
        P("local", None),
        P("local", None),
        P("local", None),
        P("local", None),
        P("local", None, "node"),
        P("local", None, "node"),
        P("local", "node", None),
    )
    return jax.shard_map(
        on_device,
        mesh=mesh,
        in_specs=placed,
        out_specs=(
            P("local", "node"),
            P("local", None),
            P("local", None, "node"),
            P("local", None, "node"),
            P("local", "node", None),
        ),
        check_vma=False,
    )
```

```python
import functools

import jax
import jax.numpy as jnp
from jax import lax
from jax.experimental import pallas as pl
from jax.experimental.pallas import tpu as pltpu
from jax.sharding import PartitionSpec as P

MESH = pl.DeviceIdType.MESH
F32 = jnp.float32
BF16 = jnp.bfloat16
TOK = 256
FEAT = 3584
QUART = FEAT // 4
HID = 256
CAP = 64
ROWS = 16 * CAP
CHUNK = 4 * CAP
HALF = CHUNK // 2
WIN = 512
TILE = 512

OFFSETS = (
    ((0, 1), (0, 3), (1, 0), (3, 0)),
    ((1, 1), (3, 3), (1, 3), (3, 1)),
    ((1, 2), (3, 2), (2, 1), (2, 3)),
    ((0, 0), (2, 2), (2, 0), (0, 2)),
)
SELF = (3, 0)


def dot(a, b, dims):
    return lax.dot_general(a, b, (dims, ((), ())), preferred_element_type=F32)


def eye(size):
    return lax.broadcasted_iota(jnp.int32, (size, size), 0) == lax.broadcasted_iota(jnp.int32, (size, size), 1)


def column(row):
    return jnp.sum(jnp.where(eye(TOK), row, 0.0), axis=1, keepdims=True)


def as_row(col):
    return jnp.sum(jnp.where(eye(TOK), col, 0.0), axis=0, keepdims=True)


def kernel(
    saved, ograd, routes, gates, gate_w, up_w, down_w,
    gin_o, gg_o, ggu_o, gdw_o,
    tok, send, onehot, gsend, grecv, xy, w, wd, grad_pre, hidden, part,
    sib_in, z_in, ret, back, gt_send, gt_recv, gt_sib, gt_mine, gt_z,
    comb, comb_sib, opp_out, opp_in, stage_gu, stage_d,
    load_sem, disp_send, disp_recv, gate_send, gate_recv, fz_send, fz_recv, fs_send, fs_recv,
    sib_send, sib_recv, zr_send, zr_recv, ret_send, ret_recv, gts_send, gts_recv, gtx_send, gtx_recv,
    gtz_send, gtz_recv, cs_send, cs_recv, op_send, op_recv, out_sem,
):
    n, l = lax.axis_index("node"), lax.axis_index("local")
    z, c = lax.div(n, 2), lax.rem(n, 2)
    x, y = lax.div(l, 4), lax.rem(l, 4)
    other = 1 - c

    def plane(dx, dy):
        return (n, lax.rem(x + dx, 4) * 4 + lax.rem(y + dy, 4))

    def along_z(dz):
        return (lax.rem(z + dz, 4) * 2 + c, l)

    sibling = (z * 2 + other, l)

    def quarter(dz):
        return pl.ds(pl.multiple_of(lax.rem(z + dz, 4) * QUART, 128), QUART)

    def rows(start, size):
        return pl.ds(pl.multiple_of(start, size), size)

    def wait(ref, sem):
        pltpu.make_async_copy(ref, ref, sem).wait()

    def push(src, dst, send_sem, recv_sem, device):
        pltpu.make_async_remote_copy(
            src_ref=src, dst_ref=dst, send_sem=send_sem, recv_sem=recv_sem,
            device_id=device, device_id_type=MESH,
        ).start()

    barrier = pltpu.get_barrier_semaphore()
    for dx in range(4):
        for dy in range(4):
            if (dx, dy) != (0, 0):
                pl.semaphore_signal(barrier, inc=1, device_id=plane(dx, dy), device_id_type=MESH)
    for dz in (1, 2, 3):
        pl.semaphore_signal(barrier, inc=1, device_id=along_z(dz), device_id_type=MESH)
    pl.semaphore_signal(barrier, inc=1, device_id=sibling, device_id_type=MESH)

    for h in (0, 1):
        place = tok.at[:, pl.ds(h * QUART, QUART)]

        @pl.when(c == 0)
        def _():
            pltpu.make_async_copy(saved.at[:, quarter(h)], place, load_sem.at[0]).start()

        @pl.when(c == 1)
        def _():
            pltpu.make_async_copy(ograd.at[:, quarter(h)], place, load_sem.at[0]).start()

    pltpu.make_async_copy(gate_w, w.at[:, pl.ds(0, HID)], load_sem.at[1]).start()
    pltpu.make_async_copy(up_w, w.at[:, pl.ds(HID, HID)], load_sem.at[1]).start()
    pltpu.make_async_copy(down_w, wd, load_sem.at[2]).start()

    route0, route1 = column(routes[0:1, :].astype(F32)), column(routes[1:2, :].astype(F32))
    gate0, gate1 = column(gates[0:1, :].astype(F32)), column(gates[1:2, :].astype(F32))
    expert_lane = lax.broadcasted_iota(jnp.int32, (TOK, 128), 1).astype(F32)
    first = jnp.where(route0 == expert_lane, 1.0, 0.0)
    second = jnp.where(route1 == expert_lane, 1.0, 0.0)
    lower = jnp.where(
        lax.broadcasted_iota(jnp.int32, (TOK, TOK), 1) < lax.broadcasted_iota(jnp.int32, (TOK, TOK), 0), 1.0, 0.0
    ).astype(BF16)
    earlier = dot(lower, (first + second).astype(BF16), ((1,), (0,)))
    target0 = route0 * CAP + jnp.sum(earlier * first, axis=1, keepdims=True)
    target1 = route1 * CAP + jnp.sum(earlier * second, axis=1, keepdims=True)

    def slot_numbers(j):
        lane = lax.broadcasted_iota(jnp.int32, (1, CHUNK), 1)
        which, number = lax.div(lane, CAP), lax.rem(lane, CAP)
        for i, (dx, dy) in enumerate(OFFSETS[j]):
            expert = lax.rem(x + dx, 4) * 4 + lax.rem(y + dy, 4)
            number = number + jnp.where(which == i, expert * CAP, 0)
        return number.astype(F32)

    def mark(j):
        number = slot_numbers(j)
        hit0, hit1 = target0 == number, target1 == number
        onehot[:, j * CHUNK:(j + 1) * CHUNK] = jnp.where(hit0 | hit1, 1.0, 0.0).astype(BF16)
        weight = jnp.where(hit0, gate0, 0.0) + jnp.where(hit1, gate1, 0.0)
        gsend[:, j * CHUNK:(j + 1) * CHUNK] = jnp.broadcast_to(jnp.sum(weight, axis=0, keepdims=True), (8, CHUNK))

    def pick(j):
        picked = dot(onehot[:, j * CHUNK:(j + 1) * CHUNK], tok[...], ((0,), (0,)))
        send[j * CHUNK:(j + 1) * CHUNK, :] = picked.astype(BF16)

    def send_gates(j):
        for i, (dx, dy) in enumerate(OFFSETS[j]):
            tile = gsend.at[:, pl.ds(j * CHUNK + (i // 2) * 128, 128)]
            if (j, i) == SELF:
                pltpu.make_async_copy(tile, grecv.at[j * 4 + i], gate_recv).start()
            else:
                push(tile, grecv.at[j * 4 + i], gate_send, gate_recv, plane(dx, dy))

    def dispatch(j, h, p=None):
        for i, (dx, dy) in enumerate(OFFSETS[j]):
            if p is not None and i // 2 != p:
                continue
            here = pl.ds((j * 4 + i) * CAP, CAP)
            src, dst = send.at[here, pl.ds(h * QUART, QUART)], xy.at[c, here, quarter(h)]
            rsem = disp_recv.at[j + (p or 0), h]
            if (j, i) == SELF:
                pltpu.make_async_copy(src, dst, rsem).start()
            else:
                push(src, dst, disp_send, rsem, plane(dx, dy))

    def forward(j, h, p=None):
        here = pl.ds(j * CHUNK, CHUNK) if p is None else pl.ds(j * CHUNK + p * HALF, HALF)
        block = xy.at[c, here, quarter(h)]
        wait(block, disp_recv.at[j + (p or 0), h])
        push(block, block, fz_send, fz_recv.at[j, h], along_z((1, 3)[h]))
        push(block, block, fs_send, fs_recv.at[j, h], sibling)

    def hand_over(j):
        here = pl.ds(j * CHUNK, CHUNK)
        for h, dz in ((0, 3), (1, 2)):
            block = xy.at[c, here, quarter(dz)]
            wait(block, fz_recv.at[j, h])
            push(block, block, fs_send, fs_recv.at[j, 2 + h], sibling)

    def compute(j):
        here = pl.ds(j * CHUNK, CHUNK)
        slot = j % 2
        for h, dz in ((0, 0), (1, 1), (2, 3), (3, 2)):
            wait(xy.at[other, here, quarter(dz)], fs_recv.at[j, h])
        lane = lax.broadcasted_iota(jnp.int32, (CAP, 128), 1)
        row = lax.broadcasted_iota(jnp.int32, (CAP, 128), 0)
        cols = []
        for i in range(4):
            values = grecv[j * 4 + i][0:1, :]
            cols.append(jnp.sum(jnp.where(lane == row + (i % 2) * CAP, values, 0.0), axis=1, keepdims=True))
        gate = jnp.concatenate(cols, axis=0)
        pre = dot(xy[0, here, :], w[...], ((1,), (0,)))
        back_proj = dot(xy[1, here, :], wd[...], ((1,), (1,)))
        gate_pre, up_pre = pre[:, :HID], pre[:, HID:]
        sig = jax.nn.sigmoid(gate_pre)
        act = gate_pre * sig
        act_up = act * up_pre
        term = jnp.sum(act_up * back_proj, axis=1, keepdims=True)
        hidden[here, :] = (gate * act_up).astype(BF16)
        hidden_grad = gate * back_proj
        grad_pre[here, 0:HID] = (hidden_grad * up_pre * sig * (1.0 + gate_pre * (1.0 - sig))).astype(BF16)
        grad_pre[here, HID:2 * HID] = (hidden_grad * act).astype(BF16)
        gt_send[:, here] = jnp.broadcast_to(as_row(term), (8, CHUNK))

        if j >= 2:
            wait(part.at[slot, pl.ds(0, HALF)], sib_send.at[slot])
            wait(part.at[slot, pl.ds(0, HALF), pl.ds(0, 2 * QUART)], zr_send.at[slot])
        for dz in (1, 3, 2, 0):
            cut = quarter(dz)
            part[slot, :, cut] = dot(grad_pre[here, :], w[cut, :], ((1,), (1,))).astype(BF16)
            push(
                part.at[slot, rows(other * HALF, HALF), cut], sib_in.at[pl.ds(j * HALF, HALF), cut],
                sib_send.at[slot], sib_recv.at[j, dz], sibling,
            )
        for i, (dx, dy) in enumerate(OFFSETS[j]):
            tile = gt_send.at[:, pl.ds(j * CHUNK + (i // 2) * 128, 128)]
            if (j, i) == SELF:
                pltpu.make_async_copy(tile, gt_recv.at[j * 4 + i], gts_recv).start()
            else:
                push(tile, gt_recv.at[j * 4 + i], gts_send, gts_recv, plane(4 - dx, 4 - dy))

    def sum_cores(j):
        slot = j % 2
        mine, here = rows(c * HALF, HALF), pl.ds(j * HALF, HALF)
        for h, dz in ((0, 1), (1, 3)):
            cut = quarter(dz)
            wait(sib_in.at[here, cut], sib_recv.at[j, dz])
            part[slot, mine, cut] = (part[slot, mine, cut].astype(F32) + sib_in[here, cut].astype(F32)).astype(BF16)
            push(part.at[slot, mine, cut], z_in.at[h, here], zr_send.at[slot], zr_recv.at[j, h], along_z(dz))
        cut = quarter(2)
        wait(sib_in.at[here, cut], sib_recv.at[j, 2])
        ret[1, here, :] = (part[slot, mine, cut].astype(F32) + sib_in[here, cut].astype(F32)).astype(BF16)
        send_back(j, 1)

    def send_back(j, s):
        for ii in (0, 1):
            (dx0, dy0), (dx1, dy1) = OFFSETS[j][ii], OFFSETS[j][2 + ii]
            device = plane(4 - dx0 + c * (dx0 - dx1), 4 - dy0 + c * (dy0 - dy1))
            here = pl.ds(j * HALF + ii * CAP, CAP)
            src, dst, rsem = ret.at[s, here], back.at[s, here], ret_recv.at[s, j]
            if (j, ii) == SELF:
                @pl.when(c == 0)
                def _():
                    pltpu.make_async_copy(src, dst, rsem).start()

                @pl.when(c == 1)
                def _():
                    push(src, dst, ret_send, rsem, device)
            else:
                push(src, dst, ret_send, rsem, device)

    def sum_planes(j):
        slot = j % 2
        mine, here = rows(c * HALF, HALF), pl.ds(j * HALF, HALF)
        cut = quarter(0)
        wait(sib_in.at[here, cut], sib_recv.at[j, 0])
        total = part[slot, mine, cut].astype(F32) + sib_in[here, cut].astype(F32)
        for h in (0, 1):
            wait(z_in.at[h, here], zr_recv.at[j, h])
        ret[0, here, :] = (total + z_in[0, here, :].astype(F32) + z_in[1, here, :].astype(F32)).astype(BF16)
        send_back(j, 0)

    def weight_grads(t):
        slot, cut = t % 2, pl.ds(t * TILE, TILE)
        if t >= 2:
            drain(slot)
        stage_gu[slot] = dot(xy[0, :, cut], grad_pre[...], ((0,), (0,))).astype(BF16)
        stage_d[slot] = dot(hidden[...], xy[1, :, cut], ((0,), (0,))).astype(BF16)
        pltpu.make_async_copy(stage_gu.at[slot], ggu_o.at[cut], out_sem.at[slot, 0]).start()
        pltpu.make_async_copy(stage_d.at[slot], gdw_o.at[:, cut], out_sem.at[slot, 1]).start()

    def drain(slot):
        wait(stage_gu.at[slot], out_sem.at[slot, 0])
        wait(stage_d.at[slot], out_sem.at[slot, 1])

    def combine(s, j):
        here = pl.ds(j * HALF, HALF)
        wait(back.at[s, here], ret_recv.at[s, j])
        total = dot(onehot[:, rows(j * CHUNK + c * HALF, HALF)], back[s, here, :], ((1,), (0,)))
        if j == 0:
            comb[s, :, :] = total
        else:
            comb[s, :, :] += total

    def window(core):
        return pl.ds(pl.multiple_of(core * (QUART - WIN), 128), WIN)

    def trade(s):
        push(comb.at[s, :, window(other)], comb_sib.at[s], cs_send.at[s], cs_recv.at[s], sibling)

    for j in range(4):
        mark(j)
    wait(tok, load_sem.at[0])
    pick(0)
    pl.semaphore_wait(barrier, 19)
    for j in range(4):
        send_gates(j)
    dispatch(0, 0)
    dispatch(0, 1)
    pick(1)
    pick(2)
    pick(3)

    forward(0, 0)
    dispatch(1, 0)
    forward(0, 1)
    dispatch(1, 1)
    forward(1, 0)
    dispatch(2, 0)
    hand_over(0)
    wait(grecv, gate_recv)
    wait(w, load_sem.at[1])
    wait(wd, load_sem.at[2])
    forward(1, 1)
    dispatch(2, 1)
    compute(0)
    forward(2, 0)
    dispatch(3, 0, 0)
    dispatch(3, 1, 0)
    sum_cores(0)
    forward(2, 1)
    hand_over(1)
    compute(1)
    forward(3, 0, 0)
    dispatch(3, 0, 1)
    sum_cores(1)
    forward(3, 1, 0)
    dispatch(3, 1, 1)
    sum_planes(0)
    hand_over(2)
    forward(3, 0, 1)
    compute(2)
    forward(3, 1, 1)
    sum_cores(2)
    sum_planes(1)
    hand_over(3)
    compute(3)
    sum_cores(3)
    sum_planes(2)
    weight_grads(0)
    weight_grads(1)
    for s in (0, 1):
        combine(s, 0)
        combine(s, 1)
    combine(1, 2)
    weight_grads(2)
    wait(gt_recv, gts_recv)
    low = lax.broadcasted_iota(jnp.int32, (8, 128), 1) < CAP
    for m in range(8):
        gt_mine[:, m * 128:(m + 1) * 128] = jnp.where(low, gt_recv[2 * m], gt_recv[2 * m + 1])
    push(gt_mine, gt_sib, gtx_send, gtx_recv, sibling)
    combine(1, 3)
    trade(1)
    sum_planes(3)
    wait(gt_sib, gtx_recv)
    gt_z[z] = gt_mine[...] + gt_sib[...]
    for dz in (1, 2, 3):
        push(gt_z.at[z], gt_z.at[z], gtz_send.at[dz], gtz_recv.at[dz], along_z(dz))
    weight_grads(3)
    weight_grads(4)
    wait(comb_sib.at[1], cs_recv.at[1])
    opp_out[...] = (comb[1, :, window(c)] + comb_sib[1]).astype(BF16)
    push(opp_out, opp_in, op_send, op_recv, along_z(2))
    combine(0, 2)
    weight_grads(5)
    combine(0, 3)
    trade(0)
    weight_grads(6)

    for dz in (1, 2, 3):
        wait(gt_z.at[lax.rem(z + 4 - dz, 4)], gtz_recv.at[dz])
    total_row = (gt_z[0] + gt_z[1] + gt_z[2] + gt_z[3])[0:1, :]
    sum0, sum1 = jnp.zeros((TOK, 1), F32), jnp.zeros((TOK, 1), F32)
    for j in range(4):
        number = slot_numbers(j)
        term = total_row[:, j * CHUNK:(j + 1) * CHUNK]
        sum0 += jnp.sum(jnp.where(target0 == number, term, 0.0), axis=1, keepdims=True)
        sum1 += jnp.sum(jnp.where(target1 == number, term, 0.0), axis=1, keepdims=True)
    gg_o[0:1, :] = as_row(sum0)
    gg_o[1:2, :] = as_row(sum1)

    wait(comb_sib.at[0], cs_recv.at[0])
    wait(opp_in, op_recv)
    result = (comb[0, :, window(c)] + comb_sib[0] + opp_in[...].astype(F32)).T.astype(BF16)

    @pl.when(c == 0)
    def _():
        gin_o[...] = result[0:QUART // 2, :]

    @pl.when(c == 1)
    def _():
        gin_o[...] = result[WIN - QUART // 2:WIN, :]

    for slot in (0, 1):
        drain(slot)
    wait(send.at[pl.ds(CAP, ROWS - CAP)], disp_send)
    wait(grecv.at[pl.ds(1, 15)], gate_send)
    wait(gt_recv.at[pl.ds(1, 15)], gts_send)
    wait(send, fz_send)
    wait(xy.at[c], fs_send)
    for slot in (0, 1):
        wait(part.at[slot, pl.ds(0, HALF)], sib_send.at[slot])
        wait(part.at[slot, pl.ds(0, HALF), pl.ds(0, 2 * QUART)], zr_send.at[slot])

    @pl.when(c == 0)
    def _():
        wait(ret.at[0, pl.ds(CAP, 512 - CAP)], ret_send)
        wait(ret.at[1, pl.ds(CAP, 512 - CAP)], ret_send)

    @pl.when(c == 1)
    def _():
        wait(ret.at[0], ret_send)
        wait(ret.at[1], ret_send)

    wait(gt_mine, gtx_send)
    for dz in (1, 2, 3):
        wait(gt_z.at[z], gtz_send.at[dz])
    for s in (0, 1):
        wait(comb_sib.at[s], cs_send.at[s])
    wait(opp_out, op_send)


def widen(gin, gg, ggu, gdw, gin_o, gg_o, ggw_o, guw_o, gdw_o, gu, d, gw, uw, dw, in_sem, out_sem):
    cuts = [pl.ds(t * TILE, TILE) for t in range(FEAT // TILE)]
    loads = []
    for t, cut in enumerate(cuts):
        pair = (
            pltpu.make_async_copy(ggu.at[cut], gu.at[cut], in_sem.at[t, 0]),
            pltpu.make_async_copy(gdw.at[:, cut], d.at[:, cut], in_sem.at[t, 1]),
        )
        for copy in pair:
            copy.start()
        loads.append(pair)
    gin_o[...] = gin[...]
    gg_o[...] = gg[...]
    stores = []
    for t, cut in enumerate(cuts):
        for copy in loads[t]:
            copy.wait()
        gw[cut, :] = gu[cut, :HID].astype(F32)
        uw[cut, :] = gu[cut, HID:].astype(F32)
        dw[:, cut] = d[:, cut].astype(F32)
        for i, (src, dst) in enumerate((
            (gw.at[cut], ggw_o.at[cut]), (uw.at[cut], guw_o.at[cut]), (dw.at[:, cut], gdw_o.at[:, cut]),
        )):
            copy = pltpu.make_async_copy(src, dst, out_sem.at[t, i])
            copy.start()
            stores.append(copy)
    for copy in stores:
        copy.wait()


def on_device(saved_input, out_grad, routes, gates, gate_weight, up_weight, down_weight):
    anywhere = pl.BlockSpec(memory_space=pl.ANY)
    vmem = pl.BlockSpec(memory_space=pltpu.VMEM)
    dma = pltpu.SemaphoreType.DMA
    scratch = [
        pltpu.VMEM((TOK, 2 * QUART), BF16),
        pltpu.VMEM((ROWS, 2 * QUART), BF16),
        pltpu.VMEM((TOK, ROWS), BF16),
        pltpu.VMEM((8, ROWS), F32),
        pltpu.VMEM((16, 8, 128), F32),
        pltpu.VMEM((2, ROWS, FEAT), BF16),
        pltpu.VMEM((FEAT, 2 * HID), BF16),
        pltpu.VMEM((HID, FEAT), BF16),
        pltpu.VMEM((ROWS, 2 * HID), BF16),
        pltpu.VMEM((ROWS, HID), BF16),
        pltpu.VMEM((2, CHUNK, FEAT), BF16),
        pltpu.VMEM((ROWS // 2, FEAT), BF16),
        pltpu.VMEM((2, ROWS // 2, QUART), BF16),
        pltpu.VMEM((2, ROWS // 2, QUART), BF16),
        pltpu.VMEM((2, ROWS // 2, QUART), BF16),
        pltpu.VMEM((8, ROWS), F32),
        pltpu.VMEM((16, 8, 128), F32),
        pltpu.VMEM((8, ROWS), F32),
        pltpu.VMEM((8, ROWS), F32),
        pltpu.VMEM((4, 8, ROWS), F32),
        pltpu.VMEM((2, TOK, QUART), F32),
        pltpu.VMEM((2, TOK, WIN), F32),
        pltpu.VMEM((TOK, WIN), BF16),
        pltpu.VMEM((TOK, WIN), BF16),
        pltpu.VMEM((2, TILE, 2 * HID), BF16),
        pltpu.VMEM((2, HID, TILE), BF16),
        dma((3,)),
        dma(()), dma((5, 2)),
        dma(()), dma(()),
        dma(()), dma((4, 2)),
        dma(()), dma((4, 4)),
        dma((2,)), dma((4, 4)),
        dma((2,)), dma((4, 2)),
        dma(()), dma((2, 4)),
        dma(()), dma(()),
        dma(()), dma(()),
        dma((4,)), dma((4,)),
        dma((2,)), dma((2,)),
        dma(()), dma(()),
        dma((2, 2)),
    ]
    partial_outs = pl.pallas_call(
        kernel,
        out_shape=(
            jax.ShapeDtypeStruct((QUART // 2, TOK), BF16),
            jax.ShapeDtypeStruct((2, TOK), F32),
            jax.ShapeDtypeStruct((FEAT, 2 * HID), BF16),
            jax.ShapeDtypeStruct((HID, FEAT), BF16),
        ),
        in_specs=[anywhere, anywhere, vmem, vmem, anywhere, anywhere, anywhere],
        out_specs=(vmem, vmem, anywhere, anywhere),
        scratch_shapes=scratch,
        compiler_params=pltpu.CompilerParams(
            collective_id=0, has_side_effects=True, vmem_limit_bytes=62 * 2**20
        ),
        cost_estimate=pl.CostEstimate(flops=15 * 10**9, bytes_accessed=20 * 10**6, transcendentals=10**6),
    )(saved_input, out_grad, routes.T, gates.T, gate_weight[0], up_weight[0], down_weight[0])
    gin, gg, ggw, guw, gdw = pl.pallas_call(
        widen,
        out_shape=(
            jax.ShapeDtypeStruct((QUART // 2, TOK), BF16),
            jax.ShapeDtypeStruct((2, TOK), F32),
            jax.ShapeDtypeStruct((FEAT, HID), F32),
            jax.ShapeDtypeStruct((FEAT, HID), F32),
            jax.ShapeDtypeStruct((HID, FEAT), F32),
        ),
        in_specs=[vmem, vmem, anywhere, anywhere],
        out_specs=(vmem, vmem, anywhere, anywhere, anywhere),
        scratch_shapes=[
            pltpu.VMEM((FEAT, 2 * HID), BF16), pltpu.VMEM((HID, FEAT), BF16),
            pltpu.VMEM((FEAT, HID), F32), pltpu.VMEM((FEAT, HID), F32), pltpu.VMEM((HID, FEAT), F32),
            dma((FEAT // TILE, 2)), dma((FEAT // TILE, 3)),
        ],
        compiler_params=pltpu.CompilerParams(vmem_limit_bytes=62 * 2**20),
    )(*partial_outs)
    return gin.T, gg.T, ggw[None], guw[None], gdw[None]


def solution(mesh):
    placed = (
        P("local", None),
        P("local", None),
        P("local", None),
        P("local", None),
        P("local", None, "node"),
        P("local", None, "node"),
        P("local", "node", None),
    )
    return jax.shard_map(
        on_device,
        mesh=mesh,
        in_specs=placed,
        out_specs=(
            P("local", "node"),
            P("local", None),
            P("local", None, "node"),
            P("local", None, "node"),
            P("local", "node", None),
        ),
        check_vma=False,
    )
```

```python
import functools

import jax
import jax.numpy as jnp
from jax import lax
from jax.experimental import pallas as pl
from jax.experimental.pallas import tpu as pltpu
from jax.sharding import PartitionSpec as P

MESH = pl.DeviceIdType.MESH
F32 = jnp.float32
BF16 = jnp.bfloat16
TOK = 256
FEAT = 3584
QUART = FEAT // 4
HID = 256
CAP = 64
ROWS = 16 * CAP
CHUNK = 4 * CAP
HALF = CHUNK // 2
WIN = 512
TILE = 512

OFFSETS = (
    ((0, 1), (0, 3), (1, 0), (3, 0)),
    ((1, 1), (3, 3), (1, 3), (3, 1)),
    ((1, 2), (3, 2), (2, 1), (2, 3)),
    ((0, 0), (2, 2), (2, 0), (0, 2)),
)
SELF = (3, 0)


def dot(a, b, dims):
    return lax.dot_general(a, b, (dims, ((), ())), preferred_element_type=F32)


def eye(size):
    return lax.broadcasted_iota(jnp.int32, (size, size), 0) == lax.broadcasted_iota(jnp.int32, (size, size), 1)


def column(row):
    return jnp.sum(jnp.where(eye(TOK), row, 0.0), axis=1, keepdims=True)


def as_row(col):
    return jnp.sum(jnp.where(eye(TOK), col, 0.0), axis=0, keepdims=True)


def kernel(
    saved, ograd, routes, gates, gate_w, up_w, down_w,
    gin_o, gg_o, ggu_o, gdw_o,
    tok, send, onehot, gsend, grecv, xy, w, wd, grad_pre, hidden, part,
    sib_in, z_in, ret, back, gt_send, gt_recv, gt_sib, gt_mine, gt_z,
    comb, comb_sib, opp_out, opp_in, stage_gu, stage_d,
    load_sem, disp_send, disp_recv, gate_send, gate_recv, fz_send, fz_recv, fs_send, fs_recv,
    sib_send, sib_recv, zr_send, zr_recv, ret_send, ret_recv, gts_send, gts_recv, gtx_send, gtx_recv,
    gtz_send, gtz_recv, cs_send, cs_recv, op_send, op_recv, out_sem,
):
    n, l = lax.axis_index("node"), lax.axis_index("local")
    z, c = lax.div(n, 2), lax.rem(n, 2)
    x, y = lax.div(l, 4), lax.rem(l, 4)
    other = 1 - c

    def plane(dx, dy):
        return (n, lax.rem(x + dx, 4) * 4 + lax.rem(y + dy, 4))

    def along_z(dz):
        return (lax.rem(z + dz, 4) * 2 + c, l)

    sibling = (z * 2 + other, l)

    def quarter(dz):
        return pl.ds(pl.multiple_of(lax.rem(z + dz, 4) * QUART, 128), QUART)

    def rows(start, size):
        return pl.ds(pl.multiple_of(start, size), size)

    def wait(ref, sem):
        pltpu.make_async_copy(ref, ref, sem).wait()

    def push(src, dst, send_sem, recv_sem, device):
        pltpu.make_async_remote_copy(
            src_ref=src, dst_ref=dst, send_sem=send_sem, recv_sem=recv_sem,
            device_id=device, device_id_type=MESH,
        ).start()

    barrier = pltpu.get_barrier_semaphore()
    for dx in range(4):
        for dy in range(4):
            if (dx, dy) != (0, 0):
                pl.semaphore_signal(barrier, inc=1, device_id=plane(dx, dy), device_id_type=MESH)
    for dz in (1, 2, 3):
        pl.semaphore_signal(barrier, inc=1, device_id=along_z(dz), device_id_type=MESH)
    pl.semaphore_signal(barrier, inc=1, device_id=sibling, device_id_type=MESH)

    for h in (0, 1):
        place = tok.at[:, pl.ds(h * QUART, QUART)]

        @pl.when(c == 0)
        def _():
            pltpu.make_async_copy(saved.at[:, quarter(h)], place, load_sem.at[0]).start()

        @pl.when(c == 1)
        def _():
            pltpu.make_async_copy(ograd.at[:, quarter(h)], place, load_sem.at[0]).start()

    pltpu.make_async_copy(gate_w, w.at[:, pl.ds(0, HID)], load_sem.at[1]).start()
    pltpu.make_async_copy(up_w, w.at[:, pl.ds(HID, HID)], load_sem.at[1]).start()
    pltpu.make_async_copy(down_w, wd, load_sem.at[2]).start()

    route0, route1 = column(routes[0:1, :].astype(F32)), column(routes[1:2, :].astype(F32))
    gate0, gate1 = column(gates[0:1, :].astype(F32)), column(gates[1:2, :].astype(F32))
    expert_lane = lax.broadcasted_iota(jnp.int32, (TOK, 128), 1).astype(F32)
    first = jnp.where(route0 == expert_lane, 1.0, 0.0)
    second = jnp.where(route1 == expert_lane, 1.0, 0.0)
    lower = jnp.where(
        lax.broadcasted_iota(jnp.int32, (TOK, TOK), 1) < lax.broadcasted_iota(jnp.int32, (TOK, TOK), 0), 1.0, 0.0
    ).astype(BF16)
    earlier = dot(lower, (first + second).astype(BF16), ((1,), (0,)))
    target0 = route0 * CAP + jnp.sum(earlier * first, axis=1, keepdims=True)
    target1 = route1 * CAP + jnp.sum(earlier * second, axis=1, keepdims=True)

    def slot_numbers(j):
        lane = lax.broadcasted_iota(jnp.int32, (1, CHUNK), 1)
        which, number = lax.div(lane, CAP), lax.rem(lane, CAP)
        for i, (dx, dy) in enumerate(OFFSETS[j]):
            expert = lax.rem(x + dx, 4) * 4 + lax.rem(y + dy, 4)
            number = number + jnp.where(which == i, expert * CAP, 0)
        return number.astype(F32)

    def mark(j):
        number = slot_numbers(j)
        hit0, hit1 = target0 == number, target1 == number
        onehot[:, j * CHUNK:(j + 1) * CHUNK] = jnp.where(hit0 | hit1, 1.0, 0.0).astype(BF16)
        weight = jnp.where(hit0, gate0, 0.0) + jnp.where(hit1, gate1, 0.0)
        gsend[:, j * CHUNK:(j + 1) * CHUNK] = jnp.broadcast_to(jnp.sum(weight, axis=0, keepdims=True), (8, CHUNK))

    def pick(j):
        picked = dot(onehot[:, j * CHUNK:(j + 1) * CHUNK], tok[...], ((0,), (0,)))
        send[j * CHUNK:(j + 1) * CHUNK, :] = picked.astype(BF16)

    def send_gates(j):
        for i, (dx, dy) in enumerate(OFFSETS[j]):
            tile = gsend.at[:, pl.ds(j * CHUNK + (i // 2) * 128, 128)]
            if (j, i) == SELF:
                pltpu.make_async_copy(tile, grecv.at[j * 4 + i], gate_recv).start()
            else:
                push(tile, grecv.at[j * 4 + i], gate_send, gate_recv, plane(dx, dy))

    def dispatch(j, h, p=None):
        for i, (dx, dy) in enumerate(OFFSETS[j]):
            if p is not None and i // 2 != p:
                continue
            here = pl.ds((j * 4 + i) * CAP, CAP)
            src, dst = send.at[here, pl.ds(h * QUART, QUART)], xy.at[c, here, quarter(h)]
            rsem = disp_recv.at[j + (p or 0), h]
            if (j, i) == SELF:
                pltpu.make_async_copy(src, dst, rsem).start()
            else:
                push(src, dst, disp_send, rsem, plane(dx, dy))

    def forward(j, h, p=None):
        here = pl.ds(j * CHUNK, CHUNK) if p is None else pl.ds(j * CHUNK + p * HALF, HALF)
        block = xy.at[c, here, quarter(h)]
        wait(block, disp_recv.at[j + (p or 0), h])
        push(block, block, fz_send, fz_recv.at[j, h], along_z((1, 3)[h]))
        push(block, block, fs_send, fs_recv.at[j, h], sibling)

    def hand_over(j):
        here = pl.ds(j * CHUNK, CHUNK)
        for h, dz in ((0, 3), (1, 2)):
            block = xy.at[c, here, quarter(dz)]
            wait(block, fz_recv.at[j, h])
            push(block, block, fs_send, fs_recv.at[j, 2 + h], sibling)

    def compute(j):
        here = pl.ds(j * CHUNK, CHUNK)
        slot = j
        for h, dz in ((0, 0), (1, 1), (2, 3), (3, 2)):
            wait(xy.at[other, here, quarter(dz)], fs_recv.at[j, h])
        lane = lax.broadcasted_iota(jnp.int32, (CAP, 128), 1)
        row = lax.broadcasted_iota(jnp.int32, (CAP, 128), 0)
        cols = []
        for i in range(4):
            values = grecv[j * 4 + i][0:1, :]
            cols.append(jnp.sum(jnp.where(lane == row + (i % 2) * CAP, values, 0.0), axis=1, keepdims=True))
        gate = jnp.concatenate(cols, axis=0)
        pre = dot(xy[0, here, :], w[...], ((1,), (0,)))
        back_proj = dot(xy[1, here, :], wd[...], ((1,), (1,)))
        gate_pre, up_pre = pre[:, :HID], pre[:, HID:]
        sig = jax.nn.sigmoid(gate_pre)
        act = gate_pre * sig
        act_up = act * up_pre
        term = jnp.sum(act_up * back_proj, axis=1, keepdims=True)
        hidden[here, :] = (gate * act_up).astype(BF16)
        hidden_grad = gate * back_proj
        grad_pre[here, 0:HID] = (hidden_grad * up_pre * sig * (1.0 + gate_pre * (1.0 - sig))).astype(BF16)
        grad_pre[here, HID:2 * HID] = (hidden_grad * act).astype(BF16)
        gt_send[:, here] = jnp.broadcast_to(as_row(term), (8, CHUNK))

        for dz in (1, 3, 2, 0):
            cut = quarter(dz)
            part[slot, :, cut] = dot(grad_pre[here, :], w[cut, :], ((1,), (1,))).astype(BF16)
            push(
                part.at[slot, rows(other * HALF, HALF), cut], sib_in.at[pl.ds(j * HALF, HALF), cut],
                sib_send.at[slot], sib_recv.at[j, dz], sibling,
            )
        for i, (dx, dy) in enumerate(OFFSETS[j]):
            tile = gt_send.at[:, pl.ds(j * CHUNK + (i // 2) * 128, 128)]
            if (j, i) == SELF:
                pltpu.make_async_copy(tile, gt_recv.at[j * 4 + i], gts_recv).start()
            else:
                push(tile, gt_recv.at[j * 4 + i], gts_send, gts_recv, plane(4 - dx, 4 - dy))

    def sum_cores(j):
        slot = j
        mine, here = rows(c * HALF, HALF), pl.ds(j * HALF, HALF)
        for h, dz in ((0, 1), (1, 3)):
            cut = quarter(dz)
            wait(sib_in.at[here, cut], sib_recv.at[j, dz])
            part[slot, mine, cut] = (part[slot, mine, cut].astype(F32) + sib_in[here, cut].astype(F32)).astype(BF16)
            push(part.at[slot, mine, cut], z_in.at[h, here], zr_send.at[slot], zr_recv.at[j, h], along_z(dz))
        cut = quarter(2)
        wait(sib_in.at[here, cut], sib_recv.at[j, 2])
        ret[1, here, :] = (part[slot, mine, cut].astype(F32) + sib_in[here, cut].astype(F32)).astype(BF16)
        send_back(j, 1)

    def send_back(j, s):
        for ii in (0, 1):
            (dx0, dy0), (dx1, dy1) = OFFSETS[j][ii], OFFSETS[j][2 + ii]
            device = plane(4 - dx0 + c * (dx0 - dx1), 4 - dy0 + c * (dy0 - dy1))
            here = pl.ds(j * HALF + ii * CAP, CAP)
            src, dst, rsem = ret.at[s, here], back.at[s, here], ret_recv.at[s, j]
            if (j, ii) == SELF:
                @pl.when(c == 0)
                def _():
                    pltpu.make_async_copy(src, dst, rsem).start()

                @pl.when(c == 1)
                def _():
                    push(src, dst, ret_send, rsem, device)
            else:
                push(src, dst, ret_send, rsem, device)

    def sum_planes(j):
        slot = j
        mine, here = rows(c * HALF, HALF), pl.ds(j * HALF, HALF)
        cut = quarter(0)
        wait(sib_in.at[here, cut], sib_recv.at[j, 0])
        total = part[slot, mine, cut].astype(F32) + sib_in[here, cut].astype(F32)
        for h in (0, 1):
            wait(z_in.at[h, here], zr_recv.at[j, h])
        ret[0, here, :] = (total + z_in[0, here, :].astype(F32) + z_in[1, here, :].astype(F32)).astype(BF16)
        send_back(j, 0)

    def weight_grads(t):
        slot, cut = t % 2, pl.ds(t * TILE, TILE)
        if t >= 2:
            drain(slot)
        stage_gu[slot] = dot(xy[0, :, cut], grad_pre[...], ((0,), (0,))).astype(BF16)
        stage_d[slot] = dot(hidden[...], xy[1, :, cut], ((0,), (0,))).astype(BF16)
        pltpu.make_async_copy(stage_gu.at[slot], ggu_o.at[cut], out_sem.at[slot, 0]).start()
        pltpu.make_async_copy(stage_d.at[slot], gdw_o.at[:, cut], out_sem.at[slot, 1]).start()

    def drain(slot):
        wait(stage_gu.at[slot], out_sem.at[slot, 0])
        wait(stage_d.at[slot], out_sem.at[slot, 1])

    def combine(s, j):
        here = pl.ds(j * HALF, HALF)
        wait(back.at[s, here], ret_recv.at[s, j])
        total = dot(onehot[:, rows(j * CHUNK + c * HALF, HALF)], back[s, here, :], ((1,), (0,)))
        if j == 0:
            comb[s, :, :] = total
        else:
            comb[s, :, :] += total

    def window(core):
        return pl.ds(pl.multiple_of(core * (QUART - WIN), 128), WIN)

    def trade(s):
        push(comb.at[s, :, window(other)], comb_sib.at[s], cs_send.at[s], cs_recv.at[s], sibling)

    for j in range(4):
        mark(j)
    wait(tok, load_sem.at[0])
    pick(0)
    pl.semaphore_wait(barrier, 19)
    for j in range(4):
        send_gates(j)
    dispatch(0, 0)
    dispatch(0, 1)
    pick(1)
    pick(2)
    pick(3)

    forward(0, 0)
    dispatch(1, 0)
    forward(0, 1)
    dispatch(1, 1)
    forward(1, 0)
    dispatch(2, 0)
    hand_over(0)
    wait(grecv, gate_recv)
    wait(w, load_sem.at[1])
    wait(wd, load_sem.at[2])
    forward(1, 1)
    dispatch(2, 1)
    compute(0)
    forward(2, 0)
    dispatch(3, 0, 0)
    dispatch(3, 1, 0)
    sum_cores(0)
    forward(2, 1)
    dispatch(3, 0, 1)
    dispatch(3, 1, 1)
    hand_over(1)
    compute(1)
    forward(3, 0, 0)
    forward(3, 1, 0)
    forward(3, 0, 1)
    forward(3, 1, 1)
    hand_over(2)
    compute(2)
    sum_cores(1)
    sum_planes(0)
    hand_over(3)
    sum_cores(2)
    compute(3)
    sum_cores(3)
    sum_planes(1)
    weight_grads(0)
    sum_planes(2)
    weight_grads(1)
    combine(0, 0)
    for j in range(3):
        combine(1, j)
    weight_grads(2)
    wait(gt_recv, gts_recv)
    low = lax.broadcasted_iota(jnp.int32, (8, 128), 1) < CAP
    for m in range(8):
        gt_mine[:, m * 128:(m + 1) * 128] = jnp.where(low, gt_recv[2 * m], gt_recv[2 * m + 1])
    push(gt_mine, gt_sib, gtx_send, gtx_recv, sibling)
    combine(1, 3)
    trade(1)
    sum_planes(3)
    wait(gt_sib, gtx_recv)
    gt_z[z] = gt_mine[...] + gt_sib[...]
    for dz in (1, 2, 3):
        push(gt_z.at[z], gt_z.at[z], gtz_send.at[dz], gtz_recv.at[dz], along_z(dz))
    weight_grads(3)
    weight_grads(4)
    wait(comb_sib.at[1], cs_recv.at[1])
    opp_out[...] = (comb[1, :, window(c)] + comb_sib[1]).astype(BF16)
    push(opp_out, opp_in, op_send, op_recv, along_z(2))
    combine(0, 1)
    combine(0, 2)
    weight_grads(5)
    combine(0, 3)
    trade(0)
    weight_grads(6)

    for dz in (1, 2, 3):
        wait(gt_z.at[lax.rem(z + 4 - dz, 4)], gtz_recv.at[dz])
    total_row = (gt_z[0] + gt_z[1] + gt_z[2] + gt_z[3])[0:1, :]
    sum0, sum1 = jnp.zeros((TOK, 1), F32), jnp.zeros((TOK, 1), F32)
    for j in range(4):
        number = slot_numbers(j)
        term = total_row[:, j * CHUNK:(j + 1) * CHUNK]
        sum0 += jnp.sum(jnp.where(target0 == number, term, 0.0), axis=1, keepdims=True)
        sum1 += jnp.sum(jnp.where(target1 == number, term, 0.0), axis=1, keepdims=True)
    gg_o[0:1, :] = as_row(sum0)
    gg_o[1:2, :] = as_row(sum1)

    wait(comb_sib.at[0], cs_recv.at[0])
    wait(opp_in, op_recv)
    result = (comb[0, :, window(c)] + comb_sib[0] + opp_in[...].astype(F32)).T.astype(BF16)

    @pl.when(c == 0)
    def _():
        gin_o[...] = result[0:QUART // 2, :]

    @pl.when(c == 1)
    def _():
        gin_o[...] = result[WIN - QUART // 2:WIN, :]

    for slot in (0, 1):
        drain(slot)
    wait(send.at[pl.ds(CAP, ROWS - CAP)], disp_send)
    wait(grecv.at[pl.ds(1, 15)], gate_send)
    wait(gt_recv.at[pl.ds(1, 15)], gts_send)
    wait(send, fz_send)
    wait(xy.at[c], fs_send)
    for slot in range(4):
        wait(part.at[slot, pl.ds(0, HALF)], sib_send.at[slot])
        wait(part.at[slot, pl.ds(0, HALF), pl.ds(0, 2 * QUART)], zr_send.at[slot])

    @pl.when(c == 0)
    def _():
        wait(ret.at[0, pl.ds(CAP, 512 - CAP)], ret_send)
        wait(ret.at[1, pl.ds(CAP, 512 - CAP)], ret_send)

    @pl.when(c == 1)
    def _():
        wait(ret.at[0], ret_send)
        wait(ret.at[1], ret_send)

    wait(gt_mine, gtx_send)
    for dz in (1, 2, 3):
        wait(gt_z.at[z], gtz_send.at[dz])
    for s in (0, 1):
        wait(comb_sib.at[s], cs_send.at[s])
    wait(opp_out, op_send)


def widen(gin, gg, ggu, gdw, gin_o, gg_o, ggw_o, guw_o, gdw_o, gu, d, gw, uw, dw, in_sem, out_sem):
    cuts = [pl.ds(t * TILE, TILE) for t in range(FEAT // TILE)]
    loads = []
    for t, cut in enumerate(cuts):
        pair = (
            pltpu.make_async_copy(ggu.at[cut], gu.at[cut], in_sem.at[t, 0]),
            pltpu.make_async_copy(gdw.at[:, cut], d.at[:, cut], in_sem.at[t, 1]),
        )
        for copy in pair:
            copy.start()
        loads.append(pair)
    gin_o[...] = gin[...]
    gg_o[...] = gg[...]
    stores = []
    for t, cut in enumerate(cuts):
        for copy in loads[t]:
            copy.wait()
        gw[cut, :] = gu[cut, :HID].astype(F32)
        uw[cut, :] = gu[cut, HID:].astype(F32)
        dw[:, cut] = d[:, cut].astype(F32)
        for i, (src, dst) in enumerate((
            (gw.at[cut], ggw_o.at[cut]), (uw.at[cut], guw_o.at[cut]), (dw.at[:, cut], gdw_o.at[:, cut]),
        )):
            copy = pltpu.make_async_copy(src, dst, out_sem.at[t, i])
            copy.start()
            stores.append(copy)
    for copy in stores:
        copy.wait()


def on_device(saved_input, out_grad, routes, gates, gate_weight, up_weight, down_weight):
    anywhere = pl.BlockSpec(memory_space=pl.ANY)
    vmem = pl.BlockSpec(memory_space=pltpu.VMEM)
    dma = pltpu.SemaphoreType.DMA
    scratch = [
        pltpu.VMEM((TOK, 2 * QUART), BF16),
        pltpu.VMEM((ROWS, 2 * QUART), BF16),
        pltpu.VMEM((TOK, ROWS), BF16),
        pltpu.VMEM((8, ROWS), F32),
        pltpu.VMEM((16, 8, 128), F32),
        pltpu.VMEM((2, ROWS, FEAT), BF16),
        pltpu.VMEM((FEAT, 2 * HID), BF16),
        pltpu.VMEM((HID, FEAT), BF16),
        pltpu.VMEM((ROWS, 2 * HID), BF16),
        pltpu.VMEM((ROWS, HID), BF16),
        pltpu.VMEM((4, CHUNK, FEAT), BF16),
        pltpu.VMEM((ROWS // 2, FEAT), BF16),
        pltpu.VMEM((2, ROWS // 2, QUART), BF16),
        pltpu.VMEM((2, ROWS // 2, QUART), BF16),
        pltpu.VMEM((2, ROWS // 2, QUART), BF16),
        pltpu.VMEM((8, ROWS), F32),
        pltpu.VMEM((16, 8, 128), F32),
        pltpu.VMEM((8, ROWS), F32),
        pltpu.VMEM((8, ROWS), F32),
        pltpu.VMEM((4, 8, ROWS), F32),
        pltpu.VMEM((2, TOK, QUART), F32),
        pltpu.VMEM((2, TOK, WIN), F32),
        pltpu.VMEM((TOK, WIN), BF16),
        pltpu.VMEM((TOK, WIN), BF16),
        pltpu.VMEM((2, TILE, 2 * HID), BF16),
        pltpu.VMEM((2, HID, TILE), BF16),
        dma((3,)),
        dma(()), dma((5, 2)),
        dma(()), dma(()),
        dma(()), dma((4, 2)),
        dma(()), dma((4, 4)),
        dma((4,)), dma((4, 4)),
        dma((4,)), dma((4, 2)),
        dma(()), dma((2, 4)),
        dma(()), dma(()),
        dma(()), dma(()),
        dma((4,)), dma((4,)),
        dma((2,)), dma((2,)),
        dma(()), dma(()),
        dma((2, 2)),
    ]
    partial_outs = pl.pallas_call(
        kernel,
        out_shape=(
            jax.ShapeDtypeStruct((QUART // 2, TOK), BF16),
            jax.ShapeDtypeStruct((2, TOK), F32),
            jax.ShapeDtypeStruct((FEAT, 2 * HID), BF16),
            jax.ShapeDtypeStruct((HID, FEAT), BF16),
        ),
        in_specs=[anywhere, anywhere, vmem, vmem, anywhere, anywhere, anywhere],
        out_specs=(vmem, vmem, anywhere, anywhere),
        scratch_shapes=scratch,
        compiler_params=pltpu.CompilerParams(
            collective_id=0, has_side_effects=True, vmem_limit_bytes=62 * 2**20
        ),
        cost_estimate=pl.CostEstimate(flops=15 * 10**9, bytes_accessed=20 * 10**6, transcendentals=10**6),
    )(saved_input, out_grad, routes.T, gates.T, gate_weight[0], up_weight[0], down_weight[0])
    gin, gg, ggw, guw, gdw = pl.pallas_call(
        widen,
        out_shape=(
            jax.ShapeDtypeStruct((QUART // 2, TOK), BF16),
            jax.ShapeDtypeStruct((2, TOK), F32),
            jax.ShapeDtypeStruct((FEAT, HID), F32),
            jax.ShapeDtypeStruct((FEAT, HID), F32),
            jax.ShapeDtypeStruct((HID, FEAT), F32),
        ),
        in_specs=[vmem, vmem, anywhere, anywhere],
        out_specs=(vmem, vmem, anywhere, anywhere, anywhere),
        scratch_shapes=[
            pltpu.VMEM((FEAT, 2 * HID), BF16), pltpu.VMEM((HID, FEAT), BF16),
            pltpu.VMEM((FEAT, HID), F32), pltpu.VMEM((FEAT, HID), F32), pltpu.VMEM((HID, FEAT), F32),
            dma((FEAT // TILE, 2)), dma((FEAT // TILE, 3)),
        ],
        compiler_params=pltpu.CompilerParams(vmem_limit_bytes=62 * 2**20),
    )(*partial_outs)
    return gin.T, gg.T, ggw[None], guw[None], gdw[None]


def solution(mesh):
    placed = (
        P("local", None),
        P("local", None),
        P("local", None),
        P("local", None),
        P("local", None, "node"),
        P("local", None, "node"),
        P("local", "node", None),
    )
    return jax.shard_map(
        on_device,
        mesh=mesh,
        in_specs=placed,
        out_specs=(
            P("local", "node"),
            P("local", None),
            P("local", None, "node"),
            P("local", None, "node"),
            P("local", "node", None),
        ),
        check_vma=False,
    )
```
